32 devices in a mesh: dp: 4 (over x, core), expert: 8 (over z, y).
Axes of the slice: x: 2, y: 2, z: 4, core: 2. Of those that a mesh axis runs over, the one named last changes fastest.
Arguments:
- tokens: bfloat16 [4096, 2048], P(('dp', 'expert')), may hold values from -6 to 6
- routes: int32 [4096, 2], P(('dp', 'expert')), may hold values from 0 to 15, all different within a row; in each aligned block of 128 rows (0 to 127, 128 to 255, ...) at most 20 rows name the same one
- gate_fixed: int32 [4096, 2], P(('dp', 'expert')), may hold values from 8192 to 57344
- up_weight: bfloat16 [16, 2048, 7168], P('expert', None, 'dp'), may hold values from -0.125 to 0.125
- up_mask: int32 [16, 16, 56], P('expert', None, 'dp'), may hold values 0 or 1
- down_weight: bfloat16 [16, 7168, 2048], P('expert', 'dp'), may hold values from -0.0625 to 0.0625
- down_mask: int32 [16, 56, 16], P('expert', 'dp'), may hold values 0 or 1
- threshold: int32 [16, 7168], P('expert', 'dp'), may hold values from 1 to 8
- cotangent: bfloat16 [4096, 2048], P('dp', 'expert'), may hold values from -6 to 6
Outputs:
- mixed: bfloat16 [4096, 2048], P('dp', 'expert')
- gate_grad: float32 [4096, 2], P(('dp', 'expert'))
- potential_grad: bfloat16 [640, 16, 7168], P(None, 'expert', 'dp')
The draws below stay inside these ranges and needn't reach their ends.
Inputs may be any that keep to these rules, and one draw needn't show every extreme that they name: In each aligned block of 128 rows, no expert is named by more than 20 rows, a bound that some block reaches; the two routes of a token differ.
All inputs are finite; a program needn't handle non-finite values. No bound on the sum of `up_mask` or of `down_mask` on one device may be relied on, other than what follows from the above.
Results may differ from the reference program's by a relative error of at most 0.02.
Values may be sent and summed in bfloat16 or wider, within the bound.
A program may use at most 192 MiB of HBM per device.

```python
import math
import jax
import jax.numpy as jnp
import numpy as np
from jax import lax

D = 2048
FFW = 7168
BLOCK = 128
TOK_DEV = 128
EXPERTS = 16
CAP = 20
TOKENS = 4096
N_DP = 4
N_EXPERT = 8


def with_ends(values, own_key, low, top_value):
    shape = values.shape
    index_at = [jax.random.randint(jax.random.fold_in(own_key, axis), (), 0, shape[axis]) for axis in range(len(shape))]
    values = values.at[tuple(index_at)].set(low)
    longest = shape.index(max(shape))
    index_at[longest] = (index_at[longest] + 1) % shape[longest]
    return values.at[tuple(index_at)].set(top_value)


def level_of(key, extent, shards, least, largest):
    def one(dim, parts):
        heights = jax.random.uniform(jax.random.fold_in(jax.random.fold_in(key, 6), dim), (parts,), jnp.float32, least / len(shards), largest / len(shards))
        return jnp.repeat(jnp.exp(heights), extent[dim] // parts).reshape((-1,) + (1,) * (len(extent) - dim - 1))

    level = one(*shards[0])
    for cut in shards[1:]:
        level = level * one(*cut)
    return level


def routed_block(own_key, own, number, rows, amount, top, limit, lean):
    ranking = jax.random.permutation(own_key, amount)
    heavy_load, usual = shares(amount, rows * top, limit, lean, True), shares(amount, rows * top, limit, lean, False)
    places = jnp.arange(amount)

    def named(sizes, turn):
        used = int((sizes > 0).sum())
        fixed = max(1, used // 4)
        shifted = fixed + (places - fixed + turn * (used - fixed)) % max(1, amount - fixed)
        return jnp.zeros((amount,), jnp.int32).at[ranking[jnp.where(places < fixed, places, shifted)]].set(jnp.asarray(sizes, jnp.int32))

    sizes = jnp.where(number % 4 == 0, named(heavy_load, number // 4), named(usual, number - number // 4 - 1))
    mixed = jax.random.permutation(jax.random.fold_in(own, 3), amount)
    source_of, taker = mixed[0:amount // 2 * 2:2], mixed[1:amount // 2 * 2:2]
    margin = jnp.minimum(sizes[source_of] - 1, limit - sizes[taker]) // 2
    margin = jnp.where((source_of == ranking[0]) | (taker == ranking[0]) | (sizes[taker] == 0), 0, jnp.maximum(margin, 0))
    shifted = jax.random.randint(jax.random.fold_in(own, 4), (amount // 2,), 0, 1 << 20) % (margin + 1)
    sizes = sizes.at[source_of].add(-shifted).at[taker].add(shifted)
    members = jnp.searchsorted(jnp.cumsum(sizes), jnp.arange(rows * top), side="right").astype(jnp.int32)
    grid = members.reshape(top, rows).T
    grid = grid[jax.random.permutation(jax.random.fold_in(own, 1), rows)]
    turn = jax.random.randint(jax.random.fold_in(own, 2), (rows, 1), 0, top)
    return jnp.take_along_axis(grid, (jnp.arange(top)[None, :] + turn) % top, axis=1)


def shares(count, total, bound, lean, full):
    weights = [(1 << 20) // math.isqrt(rank ** lean) + 1 for rank in range(1, count + 1)]
    largest = bound if full else min(bound, max(-(-total // count), total * weights[0] // sum(weights)))
    least = 1 if total - largest >= count - 1 else 0
    counts, surplus = [largest] + [least] * (count - 1), total - largest - least * (count - 1)
    while surplus > 0:
        candidates = [i for i in range(1, count) if counts[i] < largest] or [i for i in range(1, count) if counts[i] < bound]
        whole, budget = sum([weights[i] for i in candidates]), surplus
        for i in candidates:
            extra = min(bound - counts[i], max(1, budget * weights[i] // whole), surplus)
            counts[i] = counts[i] + extra
            surplus = surplus - extra
    return np.array(counts)


def scatter_about(own_key, shape, scale, reach, pieces=(), held_as=jnp.bfloat16):
    level = level_of(own_key, shape, pieces, -0.22, 0.18) if pieces else 1.0
    result = jax.random.normal(own_key, shape, jnp.float32) * scale * level
    return jnp.minimum(jnp.maximum(result, -reach), reach).astype(held_as)


def setup_inputs(seed: int = 0) -> dict:
    keys = jax.random.split(jax.random.key(seed), 10)
    tokens = scatter_about(keys[0], (TOKENS, D), 1.0, 6.0, ((0, 32),))
    routes_keys = jax.random.split(jax.random.fold_in(keys[1], 1), TOKENS // TOK_DEV)
    routes_turns = jax.random.permutation(jax.random.fold_in(keys[1], 3), TOKENS // TOK_DEV)
    routes = jax.vmap(lambda own, number: routed_block(jax.random.fold_in(keys[1], 2), own, number, TOK_DEV, EXPERTS, 2, CAP, 2))(routes_keys, routes_turns).reshape((TOKENS, 2))
    gate_fixed = with_ends(jax.random.randint(keys[2], (TOKENS, 2), 8192, 57345), jax.random.fold_in(keys[2], 1), 8192, 57344).astype(jnp.int32)
    up_weight = scatter_about(keys[3], (EXPERTS, D, FFW), D ** -0.5, 0.125, ((0, 8), (2, 4)))
    up_mask = with_ends((jax.random.randint(keys[4], (EXPERTS, D // BLOCK, FFW // BLOCK), 0, 4) < 3).astype(jnp.int32), jax.random.fold_in(keys[4], 1), 0, 1)
    down_weight = scatter_about(keys[5], (EXPERTS, FFW, D), FFW ** -0.5, 0.0625, ((0, 8), (1, 4)))
    down_mask = with_ends((jax.random.randint(keys[6], (EXPERTS, FFW // BLOCK, D // BLOCK), 0, 4) < 3).astype(jnp.int32), jax.random.fold_in(keys[6], 1), 0, 1)
    threshold = with_ends(jax.random.randint(keys[7], (EXPERTS, FFW), 1, 9), jax.random.fold_in(keys[7], 1), 1, 8).astype(jnp.int32)
    cotangent = scatter_about(keys[8], (TOKENS, D), 1.0, 6.0, ((0, 4), (1, 8)))
    return dict(tokens=tokens, routes=routes, gate_fixed=gate_fixed, up_weight=up_weight, up_mask=up_mask, down_weight=down_weight, down_mask=down_mask, threshold=threshold, cotangent=cotangent)


def widen(mask):
    return jnp.repeat(jnp.repeat(mask, BLOCK, axis=0), BLOCK, axis=1)

def reference(tokens, routes, gate_fixed, up_weight, up_mask, down_weight, down_mask, threshold, cotangent):
    blocks = N_DP * N_EXPERT
    flat_routes = routes.reshape(blocks, TOK_DEV * 2)
    onehot = (flat_routes[:, :, None] == jnp.arange(EXPERTS, dtype=jnp.int32)[None, None, :]).astype(jnp.int32)
    earlier = jnp.cumsum(onehot, axis=1) - onehot
    slots = lax.optimization_barrier(jnp.sum(onehot * earlier, axis=2))
    source = jnp.broadcast_to(jnp.arange(blocks, dtype=jnp.int32)[:, None], flat_routes.shape)
    place = (flat_routes * (blocks * CAP) + source * CAP + slots).reshape(-1).astype(jnp.int32)
    token_of = (jnp.arange(TOKENS * 2, dtype=jnp.int32) // 2).astype(jnp.int32)
    rows = jnp.zeros((EXPERTS * blocks * CAP, D), tokens.dtype).at[place].set(tokens[token_of])
    rows = rows.reshape(EXPERTS, blocks * CAP, D)
    scale = 4.0 / threshold.astype(jnp.float32)
    width_dp = FFW // N_DP

    def forward(args):
        x_rows, w_up, m_up, w_down, m_down, scl = args
        w_up = w_up * widen(m_up).astype(w_up.dtype)
        w_down = w_down * widen(m_down).astype(w_down.dtype)
        potential = jnp.dot(x_rows, w_up, preferred_element_type=jnp.float32)
        sig = jax.nn.sigmoid(potential)
        hidden = (potential * sig * scl[None, :]).astype(jnp.bfloat16)
        slope = (sig * (1.0 + potential * (1.0 - sig)) * scl[None, :]).astype(jnp.bfloat16)
        groups = hidden.reshape(-1, N_DP, width_dp).astype(jnp.float32)
        w_groups = w_down.reshape(N_DP, width_dp, D).astype(jnp.float32)
        part = jnp.einsum('rnf,nfd->nrd', groups, w_groups).astype(jnp.bfloat16)
        out = lax.optimization_barrier(jnp.sum(part.astype(jnp.float32), axis=0)).astype(jnp.bfloat16)
        return (out, slope)
    expert_out, slopes = lax.map(forward, (rows, up_weight, up_mask, down_weight, down_mask, scale))
    picked = expert_out.reshape(-1, D)[place].reshape(TOKENS, 2, D)
    gates = gate_fixed.astype(jnp.float32) / 65536.0
    mixed = lax.optimization_barrier(jnp.sum(gates[:, :, None] * picked.astype(jnp.float32), axis=1)).astype(jnp.bfloat16)
    cot = cotangent.astype(jnp.float32)
    gate_grad = lax.optimization_barrier(jnp.sum(cot[:, None, :] * picked.astype(jnp.float32), axis=2)) / math.sqrt(D)
    scaled = (gates[:, :, None] * cot[:, None, :]).astype(jnp.bfloat16).reshape(TOKENS * 2, D)
    grad_rows = jnp.zeros((EXPERTS * blocks * CAP, D), jnp.bfloat16).at[place].set(scaled)
    grad_rows = grad_rows.reshape(EXPERTS, blocks * CAP, D)

    def backward(args):
        g_rows, w_down, m_down, slope = args
        w_down = w_down * widen(m_down).astype(w_down.dtype)
        back = jnp.dot(g_rows, w_down.T, preferred_element_type=jnp.float32)
        return (back * slope.astype(jnp.float32)).astype(jnp.bfloat16)
    grads = lax.map(backward, (grad_rows, down_weight, down_mask, slopes))
    potential_grad = jnp.transpose(grads, (1, 0, 2))
    return (mixed, gate_grad, potential_grad)
```

```python
import functools
import math

import jax
import jax.numpy as jnp
from jax import lax
from jax.experimental import pallas as pl
from jax.experimental.pallas import tpu as pltpu
from jax.sharding import PartitionSpec as P

BLOCK = 128
CORES = 2
VMEM_LIMIT = 60 * 1024 * 1024
MESH = pl.DeviceIdType.MESH


def greet(owners, groups):
    me, mine = lax.axis_index("dp"), lax.axis_index("expert")
    turns = groups // CORES
    x, core = me // CORES, me % CORES
    barrier = pltpu.get_barrier_semaphore()

    def hail(k, carry):
        peer = lax.rem(mine + k, owners)
        pl.semaphore_signal(
            barrier, inc=1, device_id={"dp": me, "expert": peer}, device_id_type=MESH
        )
        return carry

    lax.fori_loop(1, owners, hail, 0)
    others = [x * CORES + 1 - core]
    others += [lax.rem(x + d, turns) * CORES + core for d in range(1, turns)]
    for other in others:
        pl.semaphore_signal(
            barrier, inc=1, device_id={"dp": other, "expert": mine}, device_id_type=MESH
        )
    pl.semaphore_wait(barrier, owners - 1 + len(others))


def dispatch_kernel(
    owners, groups, rows_in, cot_in, rows_out, cot_out, local, first, twin, across, landed
):
    me, mine = lax.axis_index("dp"), lax.axis_index("expert")
    turns = groups // CORES
    x, core = me // CORES, me % CORES
    other_core = x * CORES + 1 - core
    height, breadth = cot_in.shape[2], cot_in.shape[3]
    ins = (rows_in, cot_in)

    def spot(kind, group, source):
        if kind == 0:
            return rows_out.at[group * owners + source]
        top = pl.multiple_of(group * height, 16)
        return cot_out.at[
            :, pl.ds(top, height), pl.ds(pl.multiple_of(source * breadth, 128), breadth)
        ]

    def send_first(kind, k):
        peer = lax.rem(mine + k, owners)
        return pltpu.make_async_remote_copy(
            src_ref=ins[kind].at[peer],
            dst_ref=spot(kind, me, mine),
            send_sem=first.at[kind, k],
            recv_sem=landed.at[kind, me, mine],
            device_id={"dp": me, "expert": peer},
            device_id_type=MESH,
        )

    def keep(kind):
        return pltpu.make_async_copy(ins[kind].at[mine], spot(kind, me, mine), local.at[kind])

    def relay(kind, d, source):
        group = lax.rem(x + turns - d, turns) * CORES + core
        return pltpu.make_async_remote_copy(
            src_ref=spot(kind, group, source),
            dst_ref=spot(kind, group, source),
            send_sem=twin.at[kind, d, source],
            recv_sem=landed.at[kind, group, source],
            device_id={"dp": other_core, "expert": mine},
            device_id_type=MESH,
        )

    def cross(kind, d, source):
        return pltpu.make_async_remote_copy(
            src_ref=spot(kind, me, source),
            dst_ref=spot(kind, me, source),
            send_sem=across.at[kind, d, source],
            recv_sem=landed.at[kind, me, source],
            device_id={"dp": lax.rem(x + d, turns) * CORES + core, "expert": mine},
            device_id_type=MESH,
        )

    def arrival(kind, group, source):
        return pltpu.make_async_remote_copy(
            src_ref=spot(kind, group, source),
            dst_ref=spot(kind, group, source),
            send_sem=first.at[kind, 0],
            recv_sem=landed.at[kind, group, source],
            device_id={"dp": other_core, "expert": mine},
            device_id_type=MESH,
        )

    def over(low, body):
        def step(k, carry):
            body(k)
            return carry

        lax.fori_loop(low, owners, step, 0)

    greet(owners, groups)
    for kind in (0, 1):
        keep(kind).start()
        over(1, lambda k: send_first(kind, k).start())

    def pass_on(kind, source):
        for d in range(1, turns):
            cross(kind, d, source).start()
        relay(kind, 0, source).start()

    for kind in (0, 1):
        keep(kind).wait()
        pass_on(kind, mine)

        def own(k):
            source = lax.rem(mine + owners - k, owners)
            arrival(kind, me, source).wait_recv()
            pass_on(kind, source)

        over(1, own)
        for d in range(1, turns):
            group = lax.rem(x + turns - d, turns) * CORES + core

            def far(k):
                source = lax.rem(mine + owners - k, owners)
                arrival(kind, group, source).wait_recv()
                relay(kind, d, source).start()

            over(0, far)
    for kind in (0, 1):
        for d in range(turns):
            group = lax.rem(x + turns - d, turns) * CORES + 1 - core
            over(0, lambda k: arrival(kind, group, k).wait_recv())
        over(1, lambda k: send_first(kind, k).wait_send())
        for d in range(turns):
            over(0, lambda k: relay(kind, d, k).wait_send())
        for d in range(1, turns):
            over(0, lambda k: cross(kind, d, k).wait_send())


def dispatch(rows_in, cot_in, owners, groups):
    _, packed, piece = rows_in.shape
    _, experts, height, breadth = cot_in.shape
    turns = groups // CORES
    return pl.pallas_call(
        functools.partial(dispatch_kernel, owners, groups),
        out_shape=(
            jax.ShapeDtypeStruct((groups * owners, packed, piece), jnp.bfloat16),
            jax.ShapeDtypeStruct((experts, groups * height, owners * breadth), jnp.bfloat16),
        ),
        in_specs=[pl.BlockSpec(memory_space=pl.ANY)] * 2,
        out_specs=(pl.BlockSpec(memory_space=pl.ANY),) * 2,
        scratch_shapes=[
            pltpu.SemaphoreType.DMA((2,)),
            pltpu.SemaphoreType.DMA((2, owners)),
            pltpu.SemaphoreType.DMA((2, turns, owners)),
            pltpu.SemaphoreType.DMA((2, turns, owners)),
            pltpu.SemaphoreType.DMA((2, groups, owners)),
        ],
        compiler_params=pltpu.CompilerParams(
            collective_id=0, has_side_effects=True, vmem_limit_bytes=VMEM_LIMIT
        ),
        name="dispatch",
    )(rows_in, cot_in)


def return_kernel(
    owners, groups, halves, part, ret, near, sums, far, done,
    near_s, near_r, far_s, far_r, back_s, back_r, local
):
    me, mine = lax.axis_index("dp"), lax.axis_index("expert")
    turns = groups // CORES
    x, core = me // CORES, me % CORES
    other_core = x * CORES + 1 - core
    experts, _, height, width = part.shape
    rows = height // halves
    breadth = width // owners
    chunks = [(e, h) for e in range(experts) for h in range(halves)]
    order = list(range(1, turns)) + [0]

    def band(h):
        return pl.ds(h * rows, rows)

    def fold(e, h, d):
        group = lax.rem(x + d, turns) * CORES + 1 - core
        return pltpu.make_async_remote_copy(
            src_ref=part.at[e, group, band(h)],
            dst_ref=near.at[e, d, band(h)],
            send_sem=near_s.at[e, h, d],
            recv_sem=near_r.at[e, h, d],
            device_id={"dp": other_core, "expert": mine},
            device_id_type=MESH,
        )

    def cross(e, h, d):
        return pltpu.make_async_remote_copy(
            src_ref=sums.at[e, d, band(h)],
            dst_ref=far.at[e, d - 1, band(h)],
            send_sem=far_s.at[e, h, d],
            recv_sem=far_r.at[e, h, d],
            device_id={"dp": lax.rem(x + d, turns) * CORES + core, "expert": mine},
            device_id_type=MESH,
        )

    def columns(owner):
        return pl.ds(pl.multiple_of(owner * breadth, 128), breadth)

    def give(e, h, k):
        peer = lax.rem(mine + k, owners)
        return pltpu.make_async_remote_copy(
            src_ref=done.at[e, band(h), columns(peer)],
            dst_ref=ret.at[mine, e, band(h)],
            send_sem=back_s.at[e, h, k],
            recv_sem=back_r.at[e, h, mine],
            device_id={"dp": me, "expert": peer},
            device_id_type=MESH,
        )

    def keep(e, h):
        return pltpu.make_async_copy(
            done.at[e, band(h), columns(mine)], ret.at[mine, e, band(h)], local.at[e, h]
        )

    def arrival(e, h, source):
        return pltpu.make_async_remote_copy(
            src_ref=done.at[e, band(h), columns(source)],
            dst_ref=ret.at[source, e, band(h)],
            send_sem=back_s.at[e, h, 0],
            recv_sem=back_r.at[e, h, source],
            device_id={"dp": other_core, "expert": mine},
            device_id_type=MESH,
        )

    def over(body):
        def step(k, carry):
            body(k)
            return carry

        lax.fori_loop(1, owners, step, 0)

    greet(owners, groups)
    for e, h in chunks:
        for d in order:
            fold(e, h, d).start()
    for e, h in chunks:
        for d in order:
            fold(e, h, d).wait_recv()
            group = lax.rem(x + d, turns) * CORES + core
            sums[e, d, band(h)] = (
                part[e, group, band(h)].astype(jnp.float32)
                + near[e, d, band(h)].astype(jnp.float32)
            ).astype(jnp.bfloat16)
            if d > 0:
                cross(e, h, d).start()
    for e, h in chunks:
        total = sums[e, 0, band(h)].astype(jnp.float32)
        for d in range(1, turns):
            cross(e, h, d).wait_recv()
            total = total + far[e, d - 1, band(h)].astype(jnp.float32)
        done[e, band(h)] = total.astype(jnp.bfloat16)
        over(lambda k: give(e, h, k).start())
        keep(e, h).start()
    for e, h in chunks:
        keep(e, h).wait()
        over(lambda k: arrival(e, h, lax.rem(mine + k, owners)).wait_recv())
        over(lambda k: give(e, h, k).wait_send())
        for d in range(turns):
            fold(e, h, d).wait_send()
        for d in range(1, turns):
            cross(e, h, d).wait_send()


def reduce_return(part, owners):
    experts, groups, height, width = part.shape
    turns = groups // CORES
    halves = 2 if height % 32 == 0 else 1
    sems = pltpu.SemaphoreType.DMA
    return pl.pallas_call(
        functools.partial(return_kernel, owners, groups, halves),
        out_shape=jax.ShapeDtypeStruct((owners, experts, height, width // owners), jnp.bfloat16),
        in_specs=[pl.BlockSpec(memory_space=pltpu.VMEM)],
        out_specs=pl.BlockSpec(memory_space=pl.ANY),
        scratch_shapes=[
            pltpu.VMEM((experts, turns, height, width), jnp.bfloat16),
            pltpu.VMEM((experts, turns, height, width), jnp.bfloat16),
            pltpu.VMEM((experts, max(1, turns - 1), height, width), jnp.bfloat16),
            pltpu.VMEM((experts, height, width), jnp.bfloat16),
            sems((experts, halves, turns)),
            sems((experts, halves, turns)),
            sems((experts, halves, turns)),
            sems((experts, halves, turns)),
            sems((experts, halves, owners)),
            sems((experts, halves, owners)),
            sems((experts, halves)),
        ],
        compiler_params=pltpu.CompilerParams(
            collective_id=1, has_side_effects=True, vmem_limit_bytes=VMEM_LIMIT
        ),
        name="reduce_return",
    )(part)


def masked(weights, mask):
    return (weights.reshape(mask.shape[0], BLOCK, -1) * mask[:, None, :]).reshape(weights.shape)


def forward_kernel(
    span, arrived, pick, w_up, m_up, w_down, m_down, scale, part, slope, rows, total
):
    tile, tiles = pl.program_id(1), pl.num_programs(1)
    pieces, out_rows = pick.shape[1], pick.shape[2]
    piece = arrived.shape[2]

    @pl.when(tile == 0)
    def _():
        def unpack(g, carry):
            box = arrived[pl.ds(g * span, span)].reshape(-1, piece)
            for q in range(pieces):
                rows[pl.ds(pl.multiple_of(g * out_rows, 16), out_rows), q * piece:(q + 1) * piece] = jnp.dot(
                    pick[0, q], box, preferred_element_type=jnp.float32
                ).astype(jnp.bfloat16)
            return carry

        lax.fori_loop(0, arrived.shape[0] // span, unpack, 0)

    up = masked(w_up[0], m_up[0])
    potential = jnp.dot(rows[...], up, preferred_element_type=jnp.float32)
    sig = jax.nn.sigmoid(potential)
    scaled = sig * scale[0]
    hidden = (potential * scaled).astype(jnp.bfloat16)
    slope[0] = (scaled * (1.0 + potential * (1.0 - sig))).astype(jnp.bfloat16)
    down = masked(w_down[0], m_down[0, 0])
    term = jnp.dot(hidden, down, preferred_element_type=jnp.float32)

    @pl.when(tile == 0)
    def _():
        total[...] = term

    @pl.when(tile > 0)
    def _():
        total[...] += term

    @pl.when(tile == tiles - 1)
    def _():
        part[0] = total[...].astype(jnp.bfloat16)


def backward_kernel(grad, w_down, m_down, slope, out):
    down = masked(w_down[0], m_down[0, 0])
    back = lax.dot_general(
        grad[0], down, (((1,), (1,)), ((), ())), preferred_element_type=jnp.float32
    )
    out[...] = (back * slope[0].astype(jnp.float32)).astype(jnp.bfloat16)


def places(routes, experts, capacity):
    onehot = (routes[..., None] == jnp.arange(experts, dtype=jnp.int32)).astype(jnp.bfloat16)
    count = routes.shape[1]
    at = jnp.arange(count)
    earlier = jnp.einsum(
        "ab,nbe->nae",
        (at[:, None] > at[None, :]).astype(jnp.bfloat16),
        onehot,
        preferred_element_type=jnp.float32,
    )
    slot = jnp.sum(earlier * onehot.astype(jnp.float32), axis=-1).astype(jnp.int32)
    place = routes * capacity + slot
    return (place[..., None] == jnp.arange(experts * capacity, dtype=jnp.int32)).astype(jnp.bfloat16)


def shards(
    tokens, routes, gate_fixed, up_weight, up_mask, down_weight, down_mask, threshold, cotangent
):
    owners = lax.axis_size("expert")
    groups = lax.axis_size("dp")
    tok_rows, width = tokens.shape
    held, _, hidden = up_weight.shape
    experts = held * owners
    capacity = (tok_rows * 5 + 2 * experts - 1) // (2 * experts)
    blocks = owners * groups
    all_rows = blocks * capacity
    height = owners * capacity
    breadth = width // owners
    pieces = 1
    while (held * capacity * pieces) % 16:
        pieces *= 2
    piece = width // pieces
    span = 1
    while (span * capacity) % 16:
        span *= 2
    tile = 256 if hidden % 256 == 0 else BLOCK
    tiles = hidden // tile

    own = places(routes.reshape(1, -1), experts, capacity)[0]
    choose = jnp.sum(own.reshape(tok_rows, 2, owners, held * capacity), axis=1)
    rows_in = jnp.concatenate(
        [
            jnp.einsum(
                "top,td->opd",
                choose,
                tokens[:, q * piece:(q + 1) * piece],
                preferred_element_type=jnp.float32,
            ).astype(jnp.bfloat16)
            for q in range(pieces)
        ],
        axis=1,
    )

    known = lax.all_gather(
        jnp.concatenate([routes, gate_fixed], axis=1), "expert", axis=0, tiled=True
    )
    group_place = places(known[:, :2].reshape(owners, -1), experts, capacity)
    gates = known[:, 2:].astype(jnp.float32) / 65536.0
    cot = cotangent.astype(jnp.float32)
    gated = (gates[:, :, None] * cot[:, None, :]).astype(jnp.bfloat16)
    cot_in = jnp.einsum(
        "bap,bad->bpd",
        group_place,
        gated.reshape(owners, tok_rows * 2, breadth),
        preferred_element_type=jnp.float32,
    ).astype(jnp.bfloat16)
    cot_in = cot_in.reshape(owners, owners, held, capacity, breadth).transpose(1, 2, 0, 3, 4)
    cot_in = cot_in.reshape(owners, held, height, breadth)

    arrived, grad_rows = dispatch(rows_in, cot_in, owners, groups)

    sources = jnp.arange(span * pieces * held * capacity)
    slots = sources % capacity
    expert_of = sources // capacity % held
    piece_of = sources // (capacity * held) % pieces
    block_of = sources // (capacity * held * pieces)
    target = block_of * capacity + slots
    pick = (
        (expert_of == jnp.arange(held)[:, None, None, None])
        & (piece_of == jnp.arange(pieces)[:, None, None])
        & (target == jnp.arange(span * capacity)[:, None])
    ).astype(jnp.bfloat16)

    scale = (4.0 / threshold.astype(jnp.float32)).reshape(held, 1, hidden)
    wide_up = jnp.repeat(up_mask.astype(jnp.bfloat16), BLOCK, axis=2)
    wide_down = jnp.repeat(down_mask.astype(jnp.bfloat16), BLOCK, axis=2)
    wide_down = wide_down.reshape(held, tiles, tile // BLOCK, width)
    down_specs = [
        pl.BlockSpec((1, tile, width), lambda e, t: (e, t, 0)),
        pl.BlockSpec((1, 1, tile // BLOCK, width), lambda e, t: (e, t, 0, 0)),
    ]
    part, slope = pl.pallas_call(
        functools.partial(forward_kernel, span),
        grid=(held, tiles),
        out_shape=(
            jax.ShapeDtypeStruct((held, all_rows, width), jnp.bfloat16),
            jax.ShapeDtypeStruct((held, all_rows, hidden), jnp.bfloat16),
        ),
        in_specs=[
            pl.BlockSpec(arrived.shape, lambda e, t: (0, 0, 0)),
            pl.BlockSpec((1,) + pick.shape[1:], lambda e, t: (e, 0, 0, 0)),
            pl.BlockSpec((1, width, tile), lambda e, t: (e, 0, t)),
            pl.BlockSpec((1, width // BLOCK, tile), lambda e, t: (e, 0, t)),
            *down_specs,
            pl.BlockSpec((1, 1, tile), lambda e, t: (e, 0, t)),
        ],
        out_specs=(
            pl.BlockSpec((1, all_rows, width), lambda e, t: (e, 0, 0)),
            pl.BlockSpec((1, all_rows, tile), lambda e, t: (e, 0, t)),
        ),
        scratch_shapes=[
            pltpu.VMEM((all_rows, width), jnp.bfloat16),
            pltpu.VMEM((all_rows, width), jnp.float32),
        ],
        compiler_params=pltpu.CompilerParams(vmem_limit_bytes=VMEM_LIMIT),
        name="forward",
    )(arrived, pick, up_weight, wide_up, down_weight, wide_down, scale)

    ret = reduce_return(part.reshape(held, groups, height, width), owners)

    potential_grad = pl.pallas_call(
        backward_kernel,
        grid=(held, tiles),
        out_shape=jax.ShapeDtypeStruct((all_rows, held * hidden), jnp.bfloat16),
        in_specs=[
            pl.BlockSpec((1, all_rows, width), lambda e, t: (e, 0, 0)),
            *down_specs,
            pl.BlockSpec((1, all_rows, tile), lambda e, t: (e, 0, t)),
        ],
        out_specs=pl.BlockSpec((all_rows, tile), lambda e, t: (0, e * tiles + t)),
        compiler_params=pltpu.CompilerParams(vmem_limit_bytes=VMEM_LIMIT),
        name="backward",
    )(grad_rows, down_weight, wide_down, slope).reshape(all_rows, held, hidden)

    by_block = ret.reshape(owners, held, owners, capacity, breadth).transpose(2, 0, 1, 3, 4)
    picked = jnp.einsum(
        "bap,bpd->bad",
        group_place,
        by_block.reshape(owners, experts * capacity, breadth),
        preferred_element_type=jnp.float32,
    ).reshape(owners * tok_rows, 2, breadth)
    mixed = jnp.sum(gates[:, :, None] * picked, axis=1).astype(jnp.bfloat16)
    gate_part = jnp.sum(cot[:, None, :] * picked, axis=2)
    gate_grad = lax.psum_scatter(gate_part, "expert", scatter_dimension=0, tiled=True)
    return (mixed, gate_grad * (1.0 / math.sqrt(width)), potential_grad)


def solution(mesh):
    placed = (
        P(("dp", "expert"), None),
        P(("dp", "expert"), None),
        P(("dp", "expert"), None),
        P("expert", None, "dp"),
        P("expert", None, "dp"),
        P("expert", "dp", None),
        P("expert", "dp", None),
        P("expert", "dp"),
        P("dp", "expert"),
    )
    return jax.shard_map(
        shards,
        mesh=mesh,
        in_specs=placed,
        out_specs=(P("dp", "expert"), P(("dp", "expert"), None), P(None, "expert", "dp")),
        check_vma=False,
    )
```

```python
import functools
import math

import jax
import jax.numpy as jnp
from jax import lax
from jax.experimental import pallas as pl
from jax.experimental.pallas import tpu as pltpu
from jax.sharding import PartitionSpec as P

BLOCK = 128
CORES = 2
VMEM_LIMIT = 60 * 1024 * 1024
MESH = pl.DeviceIdType.MESH


def greet(owners, groups):
    me, mine = lax.axis_index("dp"), lax.axis_index("expert")
    turns = groups // CORES
    x, core = me // CORES, me % CORES
    barrier = pltpu.get_barrier_semaphore()

    def hail(k, carry):
        peer = lax.rem(mine + k, owners)
        pl.semaphore_signal(
            barrier, inc=1, device_id={"dp": me, "expert": peer}, device_id_type=MESH
        )
        return carry

    lax.fori_loop(1, owners, hail, 0)
    others = [x * CORES + 1 - core]
    others += [lax.rem(x + d, turns) * CORES + core for d in range(1, turns)]
    for other in others:
        pl.semaphore_signal(
            barrier, inc=1, device_id={"dp": other, "expert": mine}, device_id_type=MESH
        )
    pl.semaphore_wait(barrier, owners - 1 + len(others))


def dispatch_kernel(
    owners, groups, span, tile, rows_in, cot_in, pick, w_up, m_up, w_down, m_down, scale,
    cot_out, part, slope, rows_out, rows, total, local, first, twin, across, landed
):
    me, mine = lax.axis_index("dp"), lax.axis_index("expert")
    turns = groups // CORES
    x, core = me // CORES, me % CORES
    other_core = x * CORES + 1 - core
    height, breadth = cot_in.shape[2], cot_in.shape[3]
    ins = (rows_in, cot_in)

    def spot(kind, group, source):
        if kind == 0:
            return rows_out.at[group * owners + source]
        top = pl.multiple_of(group * height, 16)
        return cot_out.at[
            :, pl.ds(top, height), pl.ds(pl.multiple_of(source * breadth, 128), breadth)
        ]

    def send_first(kind, k):
        peer = lax.rem(mine + k, owners)
        return pltpu.make_async_remote_copy(
            src_ref=ins[kind].at[peer],
            dst_ref=spot(kind, me, mine),
            send_sem=first.at[kind, k],
            recv_sem=landed.at[kind, me, mine],
            device_id={"dp": me, "expert": peer},
            device_id_type=MESH,
        )

    def keep(kind):
        return pltpu.make_async_copy(ins[kind].at[mine], spot(kind, me, mine), local.at[kind])

    def relay(kind, d, source):
        group = lax.rem(x + turns - d, turns) * CORES + core
        return pltpu.make_async_remote_copy(
            src_ref=spot(kind, group, source),
            dst_ref=spot(kind, group, source),
            send_sem=twin.at[kind, d, source],
            recv_sem=landed.at[kind, group, source],
            device_id={"dp": other_core, "expert": mine},
            device_id_type=MESH,
        )

    def cross(kind, d, source):
        return pltpu.make_async_remote_copy(
            src_ref=spot(kind, me, source),
            dst_ref=spot(kind, me, source),
            send_sem=across.at[kind, d, source],
            recv_sem=landed.at[kind, me, source],
            device_id={"dp": lax.rem(x + d, turns) * CORES + core, "expert": mine},
            device_id_type=MESH,
        )

    def arrival(kind, group, source):
        return pltpu.make_async_remote_copy(
            src_ref=spot(kind, group, source),
            dst_ref=spot(kind, group, source),
            send_sem=first.at[kind, 0],
            recv_sem=landed.at[kind, group, source],
            device_id={"dp": other_core, "expert": mine},
            device_id_type=MESH,
        )

    def over(low, body):
        def step(k, carry):
            body(k)
            return carry

        lax.fori_loop(low, owners, step, 0)

    greet(owners, groups)
    for kind in (0, 1):
        keep(kind).start()
        over(1, lambda k: send_first(kind, k).start())

    def pass_on(kind, source):
        for d in range(1, turns):
            cross(kind, d, source).start()
        relay(kind, 0, source).start()

    def own(kind, k):
        source = lax.rem(mine + owners - k, owners)
        arrival(kind, me, source).wait_recv()
        pass_on(kind, source)

    def far(kind, d, k):
        group = lax.rem(x + turns - d, turns) * CORES + core
        source = lax.rem(mine + owners - k, owners)
        arrival(kind, group, source).wait_recv()
        relay(kind, d, source).start()

    def last(kind):
        for d in range(turns):
            group = lax.rem(x + turns - d, turns) * CORES + 1 - core
            over(0, lambda k: arrival(kind, group, k).wait_recv())

    keep(0).wait()
    pass_on(0, mine)
    over(1, lambda k: own(0, k))
    for d in range(1, turns):
        over(0, lambda k: far(0, d, k))
    last(0)
    keep(1).wait()
    pass_on(1, mine)

    held, _, hidden = w_up.shape
    tiles = hidden // tile
    steps = held * tiles

    def body(pick, w_up, m_up, w_down, m_down, scale, part, slope):
        step = pl.program_id(0) * tiles + pl.program_id(1)

        @pl.when((step >= 1) & (step < owners))
        def _():
            own(1, step)

        forward_step(
            pl.program_id(1), tiles, span, rows_out, pick, w_up, m_up, w_down, m_down, scale,
            part, slope, rows, total,
        )

    width = w_up.shape[1]
    all_rows = rows.shape[0]
    pltpu.emit_pipeline(
        body,
        grid=(held, tiles),
        in_specs=[
            pl.BlockSpec((1,) + pick.shape[1:], lambda e, t: (e, 0, 0, 0)),
            pl.BlockSpec((1, width, tile), lambda e, t: (e, 0, t)),
            pl.BlockSpec((1, width // BLOCK, tile), lambda e, t: (e, 0, t)),
            pl.BlockSpec((1, tile, width), lambda e, t: (e, t, 0)),
            pl.BlockSpec((1, 1, tile // BLOCK, width), lambda e, t: (e, t, 0, 0)),
            pl.BlockSpec((1, 1, tile), lambda e, t: (e, 0, t)),
        ],
        out_specs=[
            pl.BlockSpec((1, all_rows, width), lambda e, t: (e, 0, 0)),
            pl.BlockSpec((1, all_rows, tile), lambda e, t: (e, 0, t)),
        ],
    )(pick, w_up, m_up, w_down, m_down, scale, part, slope)

    if steps < owners:
        lax.fori_loop(steps, owners, lambda k, c: (own(1, k), c)[1], 0)
    for d in range(1, turns):
        over(0, lambda k: far(1, d, k))
    last(1)
    for kind in (0, 1):
        over(1, lambda k: send_first(kind, k).wait_send())
        for d in range(turns):
            over(0, lambda k: relay(kind, d, k).wait_send())
        for d in range(1, turns):
            over(0, lambda k: cross(kind, d, k).wait_send())


def dispatch(rows_in, cot_in, pick, w_up, m_up, w_down, m_down, scale, owners, groups, span, tile):
    _, packed, piece = rows_in.shape
    _, experts, height, breadth = cot_in.shape
    turns = groups // CORES
    hidden = w_up.shape[2]
    all_rows, width = groups * height, owners * breadth
    return pl.pallas_call(
        functools.partial(dispatch_kernel, owners, groups, span, tile),
        out_shape=(
            jax.ShapeDtypeStruct((experts, all_rows, width), jnp.bfloat16),
            jax.ShapeDtypeStruct((experts, all_rows, width), jnp.bfloat16),
            jax.ShapeDtypeStruct((experts, all_rows, hidden), jnp.bfloat16),
        ),
        in_specs=[pl.BlockSpec(memory_space=pl.ANY)] * 8,
        out_specs=(pl.BlockSpec(memory_space=pl.ANY),) * 3,
        scratch_shapes=[
            pltpu.VMEM((groups * owners, packed, piece), jnp.bfloat16),
            pltpu.VMEM((all_rows, width), jnp.bfloat16),
            pltpu.VMEM((all_rows, width), jnp.float32),
            pltpu.SemaphoreType.DMA((2,)),
            pltpu.SemaphoreType.DMA((2, owners)),
            pltpu.SemaphoreType.DMA((2, turns, owners)),
            pltpu.SemaphoreType.DMA((2, turns, owners)),
            pltpu.SemaphoreType.DMA((2, groups, owners)),
        ],
        compiler_params=pltpu.CompilerParams(
            collective_id=0, has_side_effects=True, vmem_limit_bytes=VMEM_LIMIT
        ),
        name="dispatch",
    )(rows_in, cot_in, pick, w_up, m_up, w_down, m_down, scale)


def return_kernel(
    owners, groups, halves, tile, part, grad, w_down, m_down, slope, ret, out, near, sums, far, done,
    near_s, near_r, far_s, far_r, back_s, back_r, local
):
    me, mine = lax.axis_index("dp"), lax.axis_index("expert")
    turns = groups // CORES
    x, core = me // CORES, me % CORES
    other_core = x * CORES + 1 - core
    experts, _, height, width = part.shape
    rows = height // halves
    breadth = width // owners
    chunks = [(e, h) for e in range(experts) for h in range(halves)]
    order = list(range(1, turns)) + [0]

    def band(h):
        return pl.ds(h * rows, rows)

    def fold(e, h, d):
        group = lax.rem(x + d, turns) * CORES + 1 - core
        return pltpu.make_async_remote_copy(
            src_ref=part.at[e, group, band(h)],
            dst_ref=near.at[e, d, band(h)],
            send_sem=near_s.at[e, h, d],
            recv_sem=near_r.at[e, h, d],
            device_id={"dp": other_core, "expert": mine},
            device_id_type=MESH,
        )

    def cross(e, h, d):
        return pltpu.make_async_remote_copy(
            src_ref=sums.at[e, d, band(h)],
            dst_ref=far.at[e, d - 1, band(h)],
            send_sem=far_s.at[e, h, d],
            recv_sem=far_r.at[e, h, d],
            device_id={"dp": lax.rem(x + d, turns) * CORES + core, "expert": mine},
            device_id_type=MESH,
        )

    def columns(owner):
        return pl.ds(pl.multiple_of(owner * breadth, 128), breadth)

    def give(e, h, k):
        peer = lax.rem(mine + k, owners)
        return pltpu.make_async_remote_copy(
            src_ref=done.at[e, band(h), columns(peer)],
            dst_ref=ret.at[mine, e, band(h)],
            send_sem=back_s.at[e, h, k],
            recv_sem=back_r.at[e, h, mine],
            device_id={"dp": me, "expert": peer},
            device_id_type=MESH,
        )

    def keep(e, h):
        return pltpu.make_async_copy(
            done.at[e, band(h), columns(mine)], ret.at[mine, e, band(h)], local.at[e, h]
        )

    def arrival(e, h, source):
        return pltpu.make_async_remote_copy(
            src_ref=done.at[e, band(h), columns(source)],
            dst_ref=ret.at[source, e, band(h)],
            send_sem=back_s.at[e, h, 0],
            recv_sem=back_r.at[e, h, source],
            device_id={"dp": other_core, "expert": mine},
            device_id_type=MESH,
        )

    def over(body):
        def step(k, carry):
            body(k)
            return carry

        lax.fori_loop(1, owners, step, 0)

    greet(owners, groups)
    for e, h in chunks:
        for d in order:
            fold(e, h, d).start()
    def pair(e, h):
        for d in order:
            fold(e, h, d).wait_recv()
            group = lax.rem(x + d, turns) * CORES + core
            sums[e, d, band(h)] = (
                part[e, group, band(h)].astype(jnp.float32)
                + near[e, d, band(h)].astype(jnp.float32)
            ).astype(jnp.bfloat16)
            if d > 0:
                cross(e, h, d).start()

    def finish(e, h):
        total = sums[e, 0, band(h)].astype(jnp.float32)
        for d in range(1, turns):
            cross(e, h, d).wait_recv()
            total = total + far[e, d - 1, band(h)].astype(jnp.float32)
        done[e, band(h)] = total.astype(jnp.bfloat16)
        over(lambda k: give(e, h, k).start())
        keep(e, h).start()

    hidden = slope.shape[2]
    tiles = hidden // tile
    steps = experts * tiles
    duties = [(i, functools.partial(pair, *c)) for i, c in enumerate(chunks)]
    duties += [
        (min(steps - 1, 6 + 4 * i), functools.partial(finish, *c)) for i, c in enumerate(chunks)
    ]
    inside = [duty for duty in duties if duty[0] < steps - 1]
    after = [duty for duty in duties if duty[0] >= steps - 1]

    def body(grad, w_down, m_down, slope, out):
        step = pl.program_id(0) * tiles + pl.program_id(1)
        for at, act in inside:
            pl.when(step == at)(act)
        backward_kernel(grad, w_down, m_down, slope, out)

    all_rows = grad.shape[1]
    pltpu.emit_pipeline(
        body,
        grid=(experts, tiles),
        in_specs=[
            pl.BlockSpec((1, all_rows, width), lambda e, t: (e, 0, 0)),
            pl.BlockSpec((1, tile, width), lambda e, t: (e, t, 0)),
            pl.BlockSpec((1, 1, tile // BLOCK, width), lambda e, t: (e, t, 0, 0)),
            pl.BlockSpec((1, all_rows, tile), lambda e, t: (e, 0, t)),
        ],
        out_specs=[pl.BlockSpec((all_rows, tile), lambda e, t: (0, e * tiles + t))],
    )(grad, w_down, m_down, slope, out)
    for _, act in after:
        act()
    for e, h in chunks:
        keep(e, h).wait()
        over(lambda k: arrival(e, h, lax.rem(mine + k, owners)).wait_recv())
        over(lambda k: give(e, h, k).wait_send())
        for d in range(turns):
            fold(e, h, d).wait_send()
        for d in range(1, turns):
            cross(e, h, d).wait_send()


def reduce_return(part, grad, w_down, m_down, slope, owners, tile):
    experts, groups, height, width = part.shape
    turns = groups // CORES
    halves = 2 if height % 32 == 0 else 1
    sems = pltpu.SemaphoreType.DMA
    return pl.pallas_call(
        functools.partial(return_kernel, owners, groups, halves, tile),
        out_shape=(
            jax.ShapeDtypeStruct((owners, experts, height, width // owners), jnp.bfloat16),
            jax.ShapeDtypeStruct((slope.shape[1], experts * slope.shape[2]), jnp.bfloat16),
        ),
        in_specs=[pl.BlockSpec(memory_space=pltpu.VMEM)] + [pl.BlockSpec(memory_space=pl.ANY)] * 4,
        out_specs=(pl.BlockSpec(memory_space=pl.ANY),) * 2,
        scratch_shapes=[
            pltpu.VMEM((experts, turns, height, width), jnp.bfloat16),
            pltpu.VMEM((experts, turns, height, width), jnp.bfloat16),
            pltpu.VMEM((experts, max(1, turns - 1), height, width), jnp.bfloat16),
            pltpu.VMEM((experts, height, width), jnp.bfloat16),
            sems((experts, halves, turns)),
            sems((experts, halves, turns)),
            sems((experts, halves, turns)),
            sems((experts, halves, turns)),
            sems((experts, halves, owners)),
            sems((experts, halves, owners)),
            sems((experts, halves)),
        ],
        compiler_params=pltpu.CompilerParams(
            collective_id=1, has_side_effects=True, vmem_limit_bytes=VMEM_LIMIT
        ),
        name="reduce_return",
    )(part, grad, w_down, m_down, slope)


def swap_kernel(owners, give_all, mine_in, out, send, recv):
    me, mine = lax.axis_index("dp"), lax.axis_index("expert")
    barrier = pltpu.get_barrier_semaphore()

    def hail(k, carry):
        peer = lax.rem(mine + k, owners)
        pl.semaphore_signal(
            barrier, inc=1, device_id={"dp": me, "expert": peer}, device_id_type=MESH
        )
        return carry

    def copy(k, source, peer):
        return pltpu.make_async_remote_copy(
            src_ref=mine_in if give_all else mine_in.at[peer],
            dst_ref=out.at[source],
            send_sem=send.at[k],
            recv_sem=recv.at[source],
            device_id={"dp": me, "expert": peer},
            device_id_type=MESH,
        )

    def begin(k, carry):
        copy(k, mine, lax.rem(mine + k, owners)).start()
        return carry

    def end(k, carry):
        peer = lax.rem(mine + k, owners)
        copy(k, peer, peer).wait_recv()
        copy(k, mine, peer).wait_send()
        return carry

    lax.fori_loop(1, owners, hail, 0)
    pl.semaphore_wait(barrier, owners - 1)
    lax.fori_loop(1, owners, begin, 0)
    out[mine] = mine_in[...] if give_all else mine_in[mine]
    lax.fori_loop(1, owners, end, 0)


def swap(values, owners, give_all, number):
    shape = values.shape if give_all else values.shape[1:]
    return pl.pallas_call(
        functools.partial(swap_kernel, owners, give_all),
        out_shape=jax.ShapeDtypeStruct((owners,) + shape, values.dtype),
        in_specs=[pl.BlockSpec(memory_space=pltpu.VMEM)],
        out_specs=pl.BlockSpec(memory_space=pltpu.VMEM),
        scratch_shapes=[
            pltpu.SemaphoreType.DMA((owners,)),
            pltpu.SemaphoreType.DMA((owners,)),
        ],
        compiler_params=pltpu.CompilerParams(collective_id=number, has_side_effects=True),
        name="share" if give_all else "swap",
    )(values)


def masked(weights, mask):
    return (weights.reshape(mask.shape[0], BLOCK, -1) * mask[:, None, :]).reshape(weights.shape)


def forward_step(
    tile, tiles, span, arrived, pick, w_up, m_up, w_down, m_down, scale, part, slope, rows, total
):
    pieces, out_rows = pick.shape[1], pick.shape[2]
    piece = arrived.shape[2]

    @pl.when(tile == 0)
    def _():
        def unpack(g, carry):
            box = arrived[pl.ds(g * span, span)].reshape(-1, piece)
            for q in range(pieces):
                rows[pl.ds(pl.multiple_of(g * out_rows, 16), out_rows), q * piece:(q + 1) * piece] = jnp.dot(
                    pick[0, q], box, preferred_element_type=jnp.float32
                ).astype(jnp.bfloat16)
            return carry

        lax.fori_loop(0, arrived.shape[0] // span, unpack, 0)

    up = masked(w_up[0], m_up[0])
    potential = jnp.dot(rows[...], up, preferred_element_type=jnp.float32)
    sig = jax.nn.sigmoid(potential)
    scaled = sig * scale[0]
    hidden = (potential * scaled).astype(jnp.bfloat16)
    slope[0] = (scaled * (1.0 + potential * (1.0 - sig))).astype(jnp.bfloat16)
    down = masked(w_down[0], m_down[0, 0])
    term = jnp.dot(hidden, down, preferred_element_type=jnp.float32)

    @pl.when(tile == 0)
    def _():
        total[...] = term

    @pl.when(tile > 0)
    def _():
        total[...] += term

    @pl.when(tile == tiles - 1)
    def _():
        part[0] = total[...].astype(jnp.bfloat16)


def backward_kernel(grad, w_down, m_down, slope, out):
    down = masked(w_down[0], m_down[0, 0])
    back = lax.dot_general(
        grad[0], down, (((1,), (1,)), ((), ())), preferred_element_type=jnp.float32
    )
    out[...] = (back * slope[0].astype(jnp.float32)).astype(jnp.bfloat16)


def places(routes, experts, capacity):
    onehot = (routes[..., None] == jnp.arange(experts, dtype=jnp.int32)).astype(jnp.bfloat16)
    count = routes.shape[1]
    at = jnp.arange(count)
    earlier = jnp.einsum(
        "ab,nbe->nae",
        (at[:, None] > at[None, :]).astype(jnp.bfloat16),
        onehot,
        preferred_element_type=jnp.float32,
    )
    slot = jnp.sum(earlier * onehot.astype(jnp.float32), axis=-1).astype(jnp.int32)
    place = routes * capacity + slot
    return (place[..., None] == jnp.arange(experts * capacity, dtype=jnp.int32)).astype(jnp.bfloat16)


def shards(
    tokens, routes, gate_fixed, up_weight, up_mask, down_weight, down_mask, threshold, cotangent
):
    owners = lax.axis_size("expert")
    groups = lax.axis_size("dp")
    tok_rows, width = tokens.shape
    held, _, hidden = up_weight.shape
    experts = held * owners
    capacity = (tok_rows * 5 + 2 * experts - 1) // (2 * experts)
    blocks = owners * groups
    all_rows = blocks * capacity
    height = owners * capacity
    breadth = width // owners
    pieces = 1
    while (held * capacity * pieces) % 16:
        pieces *= 2
    piece = width // pieces
    span = 1
    while (span * capacity) % 16:
        span *= 2
    tile = 256 if hidden % 256 == 0 else BLOCK
    tiles = hidden // tile

    own = places(routes.reshape(1, -1), experts, capacity)[0]
    choose = jnp.sum(own.reshape(tok_rows, 2, owners, held * capacity), axis=1)
    rows_in = jnp.concatenate(
        [
            jnp.einsum(
                "top,td->opd",
                choose,
                tokens[:, q * piece:(q + 1) * piece],
                preferred_element_type=jnp.float32,
            ).astype(jnp.bfloat16)
            for q in range(pieces)
        ],
        axis=1,
    )

    known = swap(jnp.concatenate([routes, gate_fixed], axis=1).T, owners, True, 2)
    known = known.transpose(0, 2, 1).reshape(owners * tok_rows, 4)
    group_place = places(known[:, :2].reshape(owners, -1), experts, capacity)
    gates = known[:, 2:].astype(jnp.float32) / 65536.0
    cot = cotangent.astype(jnp.float32)
    gated = (gates[:, :, None] * cot[:, None, :]).astype(jnp.bfloat16)
    cot_in = jnp.einsum(
        "bap,bad->bpd",
        group_place,
        gated.reshape(owners, tok_rows * 2, breadth),
        preferred_element_type=jnp.float32,
    ).astype(jnp.bfloat16)
    cot_in = cot_in.reshape(owners, owners, held, capacity, breadth).transpose(1, 2, 0, 3, 4)
    cot_in = cot_in.reshape(owners, held, height, breadth)

    sources = jnp.arange(span * pieces * held * capacity)
    slots = sources % capacity
    expert_of = sources // capacity % held
    piece_of = sources // (capacity * held) % pieces
    block_of = sources // (capacity * held * pieces)
    target = block_of * capacity + slots
    pick = (
        (expert_of == jnp.arange(held)[:, None, None, None])
        & (piece_of == jnp.arange(pieces)[:, None, None])
        & (target == jnp.arange(span * capacity)[:, None])
    ).astype(jnp.bfloat16)

    scale = (4.0 / threshold.astype(jnp.float32)).reshape(held, 1, hidden)
    wide_up = jnp.repeat(up_mask.astype(jnp.bfloat16), BLOCK, axis=2)
    wide_down = jnp.repeat(down_mask.astype(jnp.bfloat16), BLOCK, axis=2)
    wide_down = wide_down.reshape(held, tiles, tile // BLOCK, width)
    grad_rows, part, slope = dispatch(
        rows_in, cot_in, pick, up_weight, wide_up, down_weight, wide_down, scale,
        owners, groups, span, tile,
    )
    ret, potential_grad = reduce_return(
        part.reshape(held, groups, height, width),
        grad_rows, down_weight, wide_down, slope, owners, tile,
    )
    potential_grad = potential_grad.reshape(all_rows, held, hidden)

    by_block = ret.reshape(owners, held, owners, capacity, breadth).transpose(2, 0, 1, 3, 4)
    picked = jnp.einsum(
        "bap,bpd->bad",
        group_place,
        by_block.reshape(owners, experts * capacity, breadth),
        preferred_element_type=jnp.float32,
    ).reshape(owners * tok_rows, 2, breadth)
    mixed = jnp.sum(gates[:, :, None] * picked, axis=1).astype(jnp.bfloat16)
    gate_part = jnp.sum(cot[:, None, :] * picked, axis=2)
    gate_part = gate_part.reshape(owners, tok_rows, 2).transpose(0, 2, 1)
    gate_grad = jnp.sum(swap(gate_part, owners, False, 3), axis=0).T
    return (mixed, gate_grad * (1.0 / math.sqrt(width)), potential_grad)


def solution(mesh):
    placed = (
        P(("dp", "expert"), None),
        P(("dp", "expert"), None),
        P(("dp", "expert"), None),
        P("expert", None, "dp"),
        P("expert", None, "dp"),
        P("expert", "dp", None),
        P("expert", "dp", None),
        P("expert", "dp"),
        P("dp", "expert"),
    )
    return jax.shard_map(
        shards,
        mesh=mesh,
        in_specs=placed,
        out_specs=(P("dp", "expert"), P(("dp", "expert"), None), P(None, "expert", "dp")),
        check_vma=False,
    )
```

```python
import functools
import math

import jax
import jax.numpy as jnp
import numpy as np
from jax import lax
from jax.experimental import pallas as pl
from jax.experimental.pallas import tpu as pltpu
from jax.sharding import PartitionSpec as P

BLOCK = 128
CORES = 2
VMEM_LIMIT = 60 * 1024 * 1024
MESH = pl.DeviceIdType.MESH


def greet(owners, groups):
    me, mine = lax.axis_index("dp"), lax.axis_index("expert")
    turns = groups // CORES
    x, core = me // CORES, me % CORES
    barrier = pltpu.get_barrier_semaphore()

    def hail(k, carry):
        peer = lax.rem(mine + k, owners)
        pl.semaphore_signal(
            barrier, inc=1, device_id={"dp": me, "expert": peer}, device_id_type=MESH
        )
        return carry

    lax.fori_loop(1, owners, hail, 0)
    others = [x * CORES + 1 - core]
    others += [lax.rem(x + d, turns) * CORES + core for d in range(1, turns)]
    for other in others:
        pl.semaphore_signal(
            barrier, inc=1, device_id={"dp": other, "expert": mine}, device_id_type=MESH
        )
    pl.semaphore_wait(barrier, owners - 1 + len(others))


def dispatch_kernel(
    owners, groups, span, tile, rows_in, cot_in, pick, w_up, m_up, w_down, m_down, scale,
    cot_out, part, slope, rows_out, rows, units, local, first, twin, across, landed
):
    me, mine = lax.axis_index("dp"), lax.axis_index("expert")
    turns = groups // CORES
    x, core = me // CORES, me % CORES
    other_core = x * CORES + 1 - core
    height, breadth = cot_in.shape[2], cot_in.shape[3]
    ins = (rows_in, cot_in)

    def spot(kind, group, source):
        if kind == 0:
            return rows_out.at[group * owners + source]
        top = pl.multiple_of(group * height, 16)
        return cot_out.at[
            :, pl.ds(top, height), pl.ds(pl.multiple_of(source * breadth, 128), breadth)
        ]

    def send_first(kind, k):
        peer = lax.rem(mine + k, owners)
        return pltpu.make_async_remote_copy(
            src_ref=ins[kind].at[peer],
            dst_ref=spot(kind, me, mine),
            send_sem=first.at[kind, k],
            recv_sem=landed.at[kind, me, mine],
            device_id={"dp": me, "expert": peer},
            device_id_type=MESH,
        )

    def keep(kind):
        return pltpu.make_async_copy(ins[kind].at[mine], spot(kind, me, mine), local.at[kind])

    def relay(kind, d, source):
        group = lax.rem(x + turns - d, turns) * CORES + core
        return pltpu.make_async_remote_copy(
            src_ref=spot(kind, group, source),
            dst_ref=spot(kind, group, source),
            send_sem=twin.at[kind, d, source],
            recv_sem=landed.at[kind, group, source],
            device_id={"dp": other_core, "expert": mine},
            device_id_type=MESH,
        )

    def cross(kind, d, source):
        return pltpu.make_async_remote_copy(
            src_ref=spot(kind, me, source),
            dst_ref=spot(kind, me, source),
            send_sem=across.at[kind, d, source],
            recv_sem=landed.at[kind, me, source],
            device_id={"dp": lax.rem(x + d, turns) * CORES + core, "expert": mine},
            device_id_type=MESH,
        )

    def arrival(kind, group, source):
        return pltpu.make_async_remote_copy(
            src_ref=spot(kind, group, source),
            dst_ref=spot(kind, group, source),
            send_sem=first.at[kind, 0],
            recv_sem=landed.at[kind, group, source],
            device_id={"dp": other_core, "expert": mine},
            device_id_type=MESH,
        )

    def over(low, body):
        def step(k, carry):
            body(k)
            return carry

        lax.fori_loop(low, owners, step, 0)

    greet(owners, groups)
    for kind in (0, 1):
        keep(kind).start()
        over(1, lambda k: send_first(kind, k).start())

    def pass_on(kind, source):
        for d in range(1, turns):
            cross(kind, d, source).start()
        relay(kind, 0, source).start()

    def own(kind, k):
        source = lax.rem(mine + owners - k, owners)
        arrival(kind, me, source).wait_recv()
        pass_on(kind, source)

    def far(kind, d, k):
        group = lax.rem(x + turns - d, turns) * CORES + core
        source = lax.rem(mine + owners - k, owners)
        arrival(kind, group, source).wait_recv()
        relay(kind, d, source).start()

    def last(kind):
        for d in range(turns):
            group = lax.rem(x + turns - d, turns) * CORES + 1 - core
            over(0, lambda k: arrival(kind, group, k).wait_recv())

    held, width, hidden = w_up.shape
    all_rows = rows.shape[1]
    pieces, out_rows = pick.shape[0], pick.shape[1] // held
    piece = rows_out.shape[2]
    spans = owners // span

    def unpack(group):
        def step(i, carry):
            at = group * spans + i
            box = rows_out[pl.ds(at * span, span)].reshape(-1, piece)
            top = pl.multiple_of(at * out_rows, 16)
            for q in range(pieces):
                got = jnp.dot(pick[q], box, preferred_element_type=jnp.float32)
                for e in range(held):
                    rows[e, pl.ds(top, out_rows), q * piece:(q + 1) * piece] = got[
                        e * out_rows:(e + 1) * out_rows
                    ].astype(jnp.bfloat16)
            return carry

        lax.fori_loop(0, spans, step, 0)

    keep(0).wait()
    pass_on(0, mine)
    over(1, lambda k: own(0, k))
    unpack(me)
    for d in range(1, turns):
        over(0, lambda k: far(0, d, k))
    for d in range(1, turns):
        unpack(lax.rem(x + turns - d, turns) * CORES + core)
    for d in range(turns):
        group = lax.rem(x + turns - d, turns) * CORES + 1 - core
        over(0, lambda k: arrival(0, group, k).wait_recv())
        unpack(group)
    keep(1).wait()
    pass_on(1, mine)

    tiles = hidden // tile
    steps = held * tiles

    def up_body(w_up, m_up, scale, slope):
        e, t = pl.program_id(0), pl.program_id(1)
        step = e * tiles + t

        @pl.when((step >= 1) & (step < owners))
        def _():
            own(1, step)

        up = masked(w_up[0], m_up[0])
        potential = jnp.dot(rows[e], up, preferred_element_type=jnp.float32)
        sig = jax.nn.sigmoid(potential)
        scaled = sig * scale[0]
        units[e, :, pl.ds(pl.multiple_of(t * tile, 128), tile)] = (potential * scaled).astype(
            jnp.bfloat16
        )
        slope[0] = (scaled * (1.0 + potential * (1.0 - sig))).astype(jnp.bfloat16)

    pltpu.emit_pipeline(
        up_body,
        grid=(held, tiles),
        in_specs=[
            pl.BlockSpec((1, width, tile), lambda e, t: (e, 0, t)),
            pl.BlockSpec((1, width // BLOCK, tile), lambda e, t: (e, 0, t)),
            pl.BlockSpec((1, 1, tile), lambda e, t: (e, 0, t)),
        ],
        out_specs=[pl.BlockSpec((1, all_rows, tile), lambda e, t: (e, 0, t))],
    )(w_up, m_up, scale, slope)
    if steps < owners:
        lax.fori_loop(steps, owners, lambda k, c: (own(1, k), c)[1], 0)

    wide = 512
    strips = width // wide
    relayed = min(owners, held * strips)

    def down_body(w_down, m_down, part):
        e = pl.program_id(0)
        step = e * strips + pl.program_id(1)
        if turns > 1:
            pl.when(step < relayed)(lambda: far(1, 1, step))
        down = masked(w_down[0], m_down[0])
        part[0] = jnp.dot(units[e], down, preferred_element_type=jnp.float32).astype(jnp.bfloat16)

    pltpu.emit_pipeline(
        down_body,
        grid=(held, strips),
        in_specs=[
            pl.BlockSpec((1, hidden, wide), lambda e, t: (e, 0, t)),
            pl.BlockSpec((1, hidden // BLOCK, wide), lambda e, t: (e, 0, t)),
        ],
        out_specs=[pl.BlockSpec((1, all_rows, wide), lambda e, t: (e, 0, t))],
    )(w_down, m_down, part)

    for d in range(1, turns):
        over(relayed if d == 1 else 0, lambda k: far(1, d, k))
    last(1)
    for kind in (0, 1):
        over(1, lambda k: send_first(kind, k).wait_send())
        for d in range(turns):
            over(0, lambda k: relay(kind, d, k).wait_send())
        for d in range(1, turns):
            over(0, lambda k: cross(kind, d, k).wait_send())


def dispatch(rows_in, cot_in, pick, w_up, m_up, w_down, m_down, scale, owners, groups, span, tile):
    _, packed, piece = rows_in.shape
    _, experts, height, breadth = cot_in.shape
    turns = groups // CORES
    hidden = w_up.shape[2]
    all_rows, width = groups * height, owners * breadth
    return pl.pallas_call(
        functools.partial(dispatch_kernel, owners, groups, span, tile),
        out_shape=(
            jax.ShapeDtypeStruct((experts, all_rows, width), jnp.bfloat16),
            jax.ShapeDtypeStruct((experts, all_rows, width), jnp.bfloat16),
            jax.ShapeDtypeStruct((experts, all_rows, hidden), jnp.bfloat16),
        ),
        in_specs=[pl.BlockSpec(memory_space=pl.ANY)] * 2
        + [pl.BlockSpec(memory_space=pltpu.VMEM)]
        + [pl.BlockSpec(memory_space=pl.ANY)] * 5,
        out_specs=(pl.BlockSpec(memory_space=pl.ANY),) * 3,
        scratch_shapes=[
            pltpu.VMEM((groups * owners, packed, piece), jnp.bfloat16),
            pltpu.VMEM((experts, all_rows, width), jnp.bfloat16),
            pltpu.VMEM((experts, all_rows, hidden), jnp.bfloat16),
            pltpu.SemaphoreType.DMA((2,)),
            pltpu.SemaphoreType.DMA((2, owners)),
            pltpu.SemaphoreType.DMA((2, turns, owners)),
            pltpu.SemaphoreType.DMA((2, turns, owners)),
            pltpu.SemaphoreType.DMA((2, groups, owners)),
        ],
        compiler_params=pltpu.CompilerParams(
            collective_id=0, has_side_effects=True, vmem_limit_bytes=VMEM_LIMIT
        ),
        name="dispatch",
    )(rows_in, cot_in, pick, w_up, m_up, w_down, m_down, scale)


def return_kernel(
    owners, groups, halves, tile, part, grad, w_down, m_down, slope, ret, out, near, sums, far, done,
    near_s, near_r, far_s, far_r, back_s, back_r, local
):
    me, mine = lax.axis_index("dp"), lax.axis_index("expert")
    turns = groups // CORES
    x, core = me // CORES, me % CORES
    other_core = x * CORES + 1 - core
    experts, _, height, width = part.shape
    rows = height // halves
    breadth = width // owners
    chunks = [(e, h) for e in range(experts) for h in range(halves)]
    order = list(range(1, turns)) + [0]

    def band(h):
        return pl.ds(h * rows, rows)

    def fold(e, h, d):
        group = lax.rem(x + d, turns) * CORES + 1 - core
        return pltpu.make_async_remote_copy(
            src_ref=part.at[e, group, band(h)],
            dst_ref=near.at[e, d, band(h)],
            send_sem=near_s.at[e, h, d],
            recv_sem=near_r.at[e, h, d],
            device_id={"dp": other_core, "expert": mine},
            device_id_type=MESH,
        )

    def cross(e, h, d):
        return pltpu.make_async_remote_copy(
            src_ref=sums.at[e, d, band(h)],
            dst_ref=far.at[e, d - 1, band(h)],
            send_sem=far_s.at[e, h, d],
            recv_sem=far_r.at[e, h, d],
            device_id={"dp": lax.rem(x + d, turns) * CORES + core, "expert": mine},
            device_id_type=MESH,
        )

    def columns(owner):
        return pl.ds(pl.multiple_of(owner * breadth, 128), breadth)

    def give(e, h, k):
        peer = lax.rem(mine + k, owners)
        return pltpu.make_async_remote_copy(
            src_ref=done.at[e, band(h), columns(peer)],
            dst_ref=ret.at[mine, e, band(h)],
            send_sem=back_s.at[e, h, k],
            recv_sem=back_r.at[e, h, mine],
            device_id={"dp": me, "expert": peer},
            device_id_type=MESH,
        )

    def keep(e, h):
        return pltpu.make_async_copy(
            done.at[e, band(h), columns(mine)], ret.at[mine, e, band(h)], local.at[e, h]
        )

    def arrival(e, h, source):
        return pltpu.make_async_remote_copy(
            src_ref=done.at[e, band(h), columns(source)],
            dst_ref=ret.at[source, e, band(h)],
            send_sem=back_s.at[e, h, 0],
            recv_sem=back_r.at[e, h, source],
            device_id={"dp": other_core, "expert": mine},
            device_id_type=MESH,
        )

    def over(body):
        def step(k, carry):
            body(k)
            return carry

        lax.fori_loop(1, owners, step, 0)

    greet(owners, groups)
    for e, h in chunks:
        for d in order:
            fold(e, h, d).start()
    def pair(e, h):
        for d in order:
            fold(e, h, d).wait_recv()
            group = lax.rem(x + d, turns) * CORES + core
            sums[e, d, band(h)] = (
                part[e, group, band(h)].astype(jnp.float32)
                + near[e, d, band(h)].astype(jnp.float32)
            ).astype(jnp.bfloat16)
            if d > 0:
                cross(e, h, d).start()

    def finish(e, h):
        total = sums[e, 0, band(h)].astype(jnp.float32)
        for d in range(1, turns):
            cross(e, h, d).wait_recv()
            total = total + far[e, d - 1, band(h)].astype(jnp.float32)
        done[e, band(h)] = total.astype(jnp.bfloat16)
        over(lambda k: give(e, h, k).start())
        keep(e, h).start()

    hidden = slope.shape[2]
    tiles = hidden // tile
    steps = experts * tiles
    duties = [(i, functools.partial(pair, *c)) for i, c in enumerate(chunks)]
    duties += [
        (min(steps - 1, 6 + 4 * i), functools.partial(finish, *c)) for i, c in enumerate(chunks)
    ]
    inside = [duty for duty in duties if duty[0] < steps - 1]
    after = [duty for duty in duties if duty[0] >= steps - 1]

    def body(grad, w_down, m_down, slope, out):
        step = pl.program_id(0) * tiles + pl.program_id(1)
        for at, act in inside:
            pl.when(step == at)(act)
        backward_kernel(grad, w_down, m_down, slope, out)

    all_rows = grad.shape[1]
    pltpu.emit_pipeline(
        body,
        grid=(experts, tiles),
        in_specs=[
            pl.BlockSpec((1, all_rows, width), lambda e, t: (e, 0, 0)),
            pl.BlockSpec((1, tile, width), lambda e, t: (e, t, 0)),
            pl.BlockSpec((1, 1, tile // BLOCK, width), lambda e, t: (e, t, 0, 0)),
            pl.BlockSpec((1, all_rows, tile), lambda e, t: (e, 0, t)),
        ],
        out_specs=[pl.BlockSpec((all_rows, tile), lambda e, t: (0, e * tiles + t))],
    )(grad, w_down, m_down, slope, out)
    for _, act in after:
        act()
    for e, h in chunks:
        keep(e, h).wait()
        over(lambda k: arrival(e, h, lax.rem(mine + k, owners)).wait_recv())
        over(lambda k: give(e, h, k).wait_send())
        for d in range(turns):
            fold(e, h, d).wait_send()
        for d in range(1, turns):
            cross(e, h, d).wait_send()


def reduce_return(part, grad, w_down, m_down, slope, owners, tile):
    experts, groups, height, width = part.shape
    turns = groups // CORES
    halves = 2 if height % 32 == 0 else 1
    sems = pltpu.SemaphoreType.DMA
    return pl.pallas_call(
        functools.partial(return_kernel, owners, groups, halves, tile),
        out_shape=(
            jax.ShapeDtypeStruct((owners, experts, height, width // owners), jnp.bfloat16),
            jax.ShapeDtypeStruct((slope.shape[1], experts * slope.shape[2]), jnp.bfloat16),
        ),
        in_specs=[pl.BlockSpec(memory_space=pltpu.VMEM)] + [pl.BlockSpec(memory_space=pl.ANY)] * 4,
        out_specs=(pl.BlockSpec(memory_space=pl.ANY),) * 2,
        scratch_shapes=[
            pltpu.VMEM((experts, turns, height, width), jnp.bfloat16),
            pltpu.VMEM((experts, turns, height, width), jnp.bfloat16),
            pltpu.VMEM((experts, max(1, turns - 1), height, width), jnp.bfloat16),
            pltpu.VMEM((experts, height, width), jnp.bfloat16),
            sems((experts, halves, turns)),
            sems((experts, halves, turns)),
            sems((experts, halves, turns)),
            sems((experts, halves, turns)),
            sems((experts, halves, owners)),
            sems((experts, halves, owners)),
            sems((experts, halves)),
        ],
        compiler_params=pltpu.CompilerParams(
            collective_id=1, has_side_effects=True, vmem_limit_bytes=VMEM_LIMIT
        ),
        name="reduce_return",
    )(part, grad, w_down, m_down, slope)


def swap_kernel(owners, give_all, mine_in, out, send, recv):
    me, mine = lax.axis_index("dp"), lax.axis_index("expert")
    barrier = pltpu.get_barrier_semaphore()

    def hail(k, carry):
        peer = lax.rem(mine + k, owners)
        pl.semaphore_signal(
            barrier, inc=1, device_id={"dp": me, "expert": peer}, device_id_type=MESH
        )
        return carry

    def copy(k, source, peer):
        return pltpu.make_async_remote_copy(
            src_ref=mine_in if give_all else mine_in.at[peer],
            dst_ref=out.at[source],
            send_sem=send.at[k],
            recv_sem=recv.at[source],
            device_id={"dp": me, "expert": peer},
            device_id_type=MESH,
        )

    def begin(k, carry):
        copy(k, mine, lax.rem(mine + k, owners)).start()
        return carry

    def end(k, carry):
        peer = lax.rem(mine + k, owners)
        copy(k, peer, peer).wait_recv()
        copy(k, mine, peer).wait_send()
        return carry

    lax.fori_loop(1, owners, hail, 0)
    pl.semaphore_wait(barrier, owners - 1)
    lax.fori_loop(1, owners, begin, 0)
    out[mine] = mine_in[...] if give_all else mine_in[mine]
    lax.fori_loop(1, owners, end, 0)


def swap(values, owners, give_all, number):
    shape = values.shape if give_all else values.shape[1:]
    return pl.pallas_call(
        functools.partial(swap_kernel, owners, give_all),
        out_shape=jax.ShapeDtypeStruct((owners,) + shape, values.dtype),
        in_specs=[pl.BlockSpec(memory_space=pltpu.VMEM)],
        out_specs=pl.BlockSpec(memory_space=pltpu.VMEM),
        scratch_shapes=[
            pltpu.SemaphoreType.DMA((owners,)),
            pltpu.SemaphoreType.DMA((owners,)),
        ],
        compiler_params=pltpu.CompilerParams(collective_id=number, has_side_effects=True),
        name="share" if give_all else "swap",
    )(values)


def masked(weights, mask):
    return (weights.reshape(mask.shape[0], BLOCK, -1) * mask[:, None, :]).reshape(weights.shape)


def backward_kernel(grad, w_down, m_down, slope, out):
    down = masked(w_down[0], m_down[0, 0])
    back = lax.dot_general(
        grad[0], down, (((1,), (1,)), ((), ())), preferred_element_type=jnp.float32
    )
    out[...] = (back * slope[0].astype(jnp.float32)).astype(jnp.bfloat16)


def places(routes, experts, capacity):
    names = jnp.arange(experts, dtype=jnp.int32)
    first, second = [(r[..., None] == names).astype(jnp.bfloat16) for r in routes]
    at = jnp.arange(first.shape[1])
    earlier = jnp.einsum(
        "ab,nbe->nae",
        (at[:, None] > at[None, :]).astype(jnp.bfloat16),
        first + second,
        preferred_element_type=jnp.float32,
    )
    spots = jnp.arange(experts * capacity, dtype=jnp.int32)

    def mark(route, onehot, before):
        slot = jnp.sum(before * onehot.astype(jnp.float32), axis=-1).astype(jnp.int32)
        return ((route * capacity + slot)[..., None] == spots).astype(jnp.bfloat16)

    return (
        mark(routes[0], first, earlier),
        mark(routes[1], second, earlier + first.astype(jnp.float32)),
    )


def shards(
    tokens, routes, gate_fixed, up_weight, up_mask, down_weight, down_mask, threshold, cotangent
):
    owners = lax.axis_size("expert")
    groups = lax.axis_size("dp")
    tok_rows, width = tokens.shape
    held, _, hidden = up_weight.shape
    experts = held * owners
    capacity = (tok_rows * 5 + 2 * experts - 1) // (2 * experts)
    blocks = owners * groups
    all_rows = blocks * capacity
    height = owners * capacity
    breadth = width // owners
    pieces = 1
    while (held * capacity * pieces) % 16:
        pieces *= 2
    piece = width // pieces
    span = 1
    while (span * capacity) % 16:
        span *= 2
    tile = 256 if hidden % 256 == 0 else BLOCK
    tiles = hidden // tile

    table = jnp.concatenate([routes, gate_fixed], axis=1).T
    own = places((table[None, 0], table[None, 1]), experts, capacity)
    choose = (own[0] + own[1]).reshape(tok_rows, owners, held * capacity)
    rows_in = jnp.concatenate(
        [
            jnp.einsum(
                "top,td->opd",
                choose,
                tokens[:, q * piece:(q + 1) * piece],
                preferred_element_type=jnp.float32,
            ).astype(jnp.bfloat16)
            for q in range(pieces)
        ],
        axis=1,
    )

    known = swap(table, owners, True, 2)
    marks = places((known[:, 0], known[:, 1]), experts, capacity)
    gates = [known[:, 2 + k].astype(jnp.float32)[..., None] / 65536.0 for k in range(2)]
    cot = cotangent.reshape(owners, tok_rows, breadth).astype(jnp.float32)
    cot_in = sum(
        jnp.einsum(
            "btp,btd->bpd",
            mark,
            (gate * cot).astype(jnp.bfloat16),
            preferred_element_type=jnp.float32,
        )
        for mark, gate in zip(marks, gates)
    ).astype(jnp.bfloat16)
    cot_in = cot_in.reshape(owners, owners, held, capacity, breadth).transpose(1, 2, 0, 3, 4)
    cot_in = cot_in.reshape(owners, held, height, breadth)

    sources = np.arange(span * pieces * held * capacity)
    expert_of = sources // capacity % held
    piece_of = sources // (capacity * held) % pieces
    block_of = sources // (capacity * held * pieces)
    target = (expert_of * span + block_of) * capacity + sources % capacity
    pick = jnp.asarray(
        (piece_of == np.arange(pieces)[:, None, None])
        & (target == np.arange(held * span * capacity)[:, None]),
        jnp.bfloat16,
    )

    scale = (4.0 / threshold.astype(jnp.float32)).reshape(held, 1, hidden)
    wide_up = jnp.repeat(up_mask.astype(jnp.bfloat16), BLOCK, axis=2)
    wide_down = jnp.repeat(down_mask.astype(jnp.bfloat16), BLOCK, axis=2)
    grad_rows, part, slope = dispatch(
        rows_in, cot_in, pick, up_weight, wide_up, down_weight, wide_down, scale,
        owners, groups, span, tile,
    )
    ret, potential_grad = reduce_return(
        part.reshape(held, groups, height, width),
        grad_rows, down_weight, wide_down.reshape(held, tiles, tile // BLOCK, width),
        slope, owners, tile,
    )
    potential_grad = potential_grad.reshape(all_rows, held, hidden)

    by_block = ret.reshape(owners, held, owners, capacity, breadth).transpose(2, 0, 1, 3, 4)
    by_block = by_block.reshape(owners, experts * capacity, breadth)
    picked = [
        jnp.einsum("btp,bpd->btd", mark, by_block, preferred_element_type=jnp.float32)
        for mark in marks
    ]
    mixed = (gates[0] * picked[0] + gates[1] * picked[1]).astype(jnp.bfloat16)
    mixed = mixed.reshape(owners * tok_rows, breadth)
    gate_part = jnp.stack([jnp.sum(cot * p, axis=2) for p in picked], axis=1)
    gate_grad = jnp.sum(swap(gate_part, owners, False, 3), axis=0).T
    return (mixed, gate_grad * (1.0 / math.sqrt(width)), potential_grad)


def solution(mesh):
    placed = (
        P(("dp", "expert"), None),
        P(("dp", "expert"), None),
        P(("dp", "expert"), None),
        P("expert", None, "dp"),
        P("expert", None, "dp"),
        P("expert", "dp", None),
        P("expert", "dp", None),
        P("expert", "dp"),
        P("dp", "expert"),
    )
    return jax.shard_map(
        shards,
        mesh=mesh,
        in_specs=placed,
        out_specs=(P("dp", "expert"), P(("dp", "expert"), None), P(None, "expert", "dp")),
        check_vma=False,
    )
```

```python
import functools
import math

import jax
import jax.numpy as jnp
import numpy as np
from jax import lax
from jax.experimental import pallas as pl
from jax.experimental.pallas import tpu as pltpu
from jax.sharding import PartitionSpec as P

BLOCK = 128
CORES = 2
VMEM_LIMIT = 60 * 1024 * 1024
MESH = pl.DeviceIdType.MESH


def greet(owners, groups):
    me, mine = lax.axis_index("dp"), lax.axis_index("expert")
    turns = groups // CORES
    x, core = me // CORES, me % CORES
    barrier = pltpu.get_barrier_semaphore()

    def hail(k, carry):
        peer = lax.rem(mine + k, owners)
        pl.semaphore_signal(
            barrier, inc=1, device_id={"dp": me, "expert": peer}, device_id_type=MESH
        )
        return carry

    lax.fori_loop(1, owners, hail, 0)
    others = [x * CORES + 1 - core]
    others += [lax.rem(x + d, turns) * CORES + core for d in range(1, turns)]
    for other in others:
        pl.semaphore_signal(
            barrier, inc=1, device_id={"dp": other, "expert": mine}, device_id_type=MESH
        )
    pl.semaphore_wait(barrier, owners - 1 + len(others))


def dispatch_kernel(
    owners, groups, span, tile, rows_in, cot_in, pick, w_up, m_up, w_down, m_down, scale,
    cot_out, part, slope, rows_out, rows, units, local, first, twin, across, landed
):
    me, mine = lax.axis_index("dp"), lax.axis_index("expert")
    turns = groups // CORES
    x, core = me // CORES, me % CORES
    other_core = x * CORES + 1 - core
    height, breadth = cot_in.shape[2], cot_in.shape[3]
    ins = (rows_in, cot_in)

    def spot(kind, group, source):
        if kind == 0:
            return rows_out.at[group * owners + source]
        top = pl.multiple_of(group * height, 16)
        return cot_out.at[
            :, pl.ds(top, height), pl.ds(pl.multiple_of(source * breadth, 128), breadth)
        ]

    def send_first(kind, k):
        peer = lax.rem(mine + k, owners)
        return pltpu.make_async_remote_copy(
            src_ref=ins[kind].at[peer],
            dst_ref=spot(kind, me, mine),
            send_sem=first.at[kind, k],
            recv_sem=landed.at[kind, me, mine],
            device_id={"dp": me, "expert": peer},
            device_id_type=MESH,
        )

    def keep(kind):
        return pltpu.make_async_copy(ins[kind].at[mine], spot(kind, me, mine), local.at[kind])

    def relay(kind, d, source):
        group = lax.rem(x + turns - d, turns) * CORES + core
        return pltpu.make_async_remote_copy(
            src_ref=spot(kind, group, source),
            dst_ref=spot(kind, group, source),
            send_sem=twin.at[kind, d, source],
            recv_sem=landed.at[kind, group, source],
            device_id={"dp": other_core, "expert": mine},
            device_id_type=MESH,
        )

    def cross(kind, d, source):
        return pltpu.make_async_remote_copy(
            src_ref=spot(kind, me, source),
            dst_ref=spot(kind, me, source),
            send_sem=across.at[kind, d, source],
            recv_sem=landed.at[kind, me, source],
            device_id={"dp": lax.rem(x + d, turns) * CORES + core, "expert": mine},
            device_id_type=MESH,
        )

    def arrival(kind, group, source):
        return pltpu.make_async_remote_copy(
            src_ref=spot(kind, group, source),
            dst_ref=spot(kind, group, source),
            send_sem=first.at[kind, 0],
            recv_sem=landed.at[kind, group, source],
            device_id={"dp": other_core, "expert": mine},
            device_id_type=MESH,
        )

    def over(low, body):
        def step(k, carry):
            body(k)
            return carry

        lax.fori_loop(low, owners, step, 0)

    greet(owners, groups)
    for kind in (0, 1):
        keep(kind).start()
        over(1, lambda k: send_first(kind, k).start())

    def pass_on(kind, source):
        for d in range(1, turns):
            cross(kind, d, source).start()
        relay(kind, 0, source).start()

    def own(kind, k):
        source = lax.rem(mine + owners - k, owners)
        arrival(kind, me, source).wait_recv()
        pass_on(kind, source)

    def far(kind, d, k):
        group = lax.rem(x + turns - d, turns) * CORES + core
        source = lax.rem(mine + owners - k, owners)
        arrival(kind, group, source).wait_recv()
        relay(kind, d, source).start()

    def last(kind):
        for d in range(turns):
            group = lax.rem(x + turns - d, turns) * CORES + 1 - core
            over(0, lambda k: arrival(kind, group, k).wait_recv())

    held, width, hidden = w_up.shape
    all_rows = rows.shape[1]
    pieces, out_rows = pick.shape[0], pick.shape[1] // held
    piece = rows_out.shape[2]
    spans = owners // span

    def unpack(group):
        def step(i, carry):
            at = group * spans + i
            box = rows_out[pl.ds(at * span, span)].reshape(-1, piece)
            top = pl.multiple_of(at * out_rows, 16)
            for q in range(pieces):
                got = jnp.dot(pick[q], box, preferred_element_type=jnp.float32)
                for e in range(held):
                    rows[e, pl.ds(top, out_rows), q * piece:(q + 1) * piece] = got[
                        e * out_rows:(e + 1) * out_rows
                    ].astype(jnp.bfloat16)
            return carry

        lax.fori_loop(0, spans, step, 0)

    keep(0).wait()
    pass_on(0, mine)
    over(1, lambda k: own(0, k))
    unpack(me)
    for d in range(1, turns):
        over(0, lambda k: far(0, d, k))
    for d in range(1, turns):
        unpack(lax.rem(x + turns - d, turns) * CORES + core)
    for d in range(turns):
        group = lax.rem(x + turns - d, turns) * CORES + 1 - core
        over(0, lambda k: arrival(0, group, k).wait_recv())
        unpack(group)
    keep(1).wait()
    pass_on(1, mine)

    tiles = hidden // tile
    steps = held * tiles

    def up_body(w_up, m_up, scale, slope):
        e, t = pl.program_id(0), pl.program_id(1)
        step = e * tiles + t

        @pl.when((step >= 1) & (step < owners))
        def _():
            own(1, step)

        up = masked(w_up[0], m_up[0])
        potential = jnp.dot(rows[e], up, preferred_element_type=jnp.float32)
        sig = jax.nn.sigmoid(potential)
        scaled = sig * scale[0]
        units[e, :, pl.ds(pl.multiple_of(t * tile, 128), tile)] = (potential * scaled).astype(
            jnp.bfloat16
        )
        slope[0] = (scaled * (1.0 + potential * (1.0 - sig))).astype(jnp.bfloat16)

    pltpu.emit_pipeline(
        up_body,
        grid=(held, tiles),
        in_specs=[
            pl.BlockSpec((1, width, tile), lambda e, t: (e, 0, t)),
            pl.BlockSpec((1, width // BLOCK, tile), lambda e, t: (e, 0, t)),
            pl.BlockSpec((1, 1, tile), lambda e, t: (e, 0, t)),
        ],
        out_specs=[pl.BlockSpec((1, all_rows, tile), lambda e, t: (e, 0, t))],
    )(w_up, m_up, scale, slope)
    if steps < owners:
        lax.fori_loop(steps, owners, lambda k, c: (own(1, k), c)[1], 0)

    wide = 512
    strips = width // wide
    relayed = min(owners, held * strips)

    def down_body(w_down, m_down, part):
        e = pl.program_id(0)
        step = e * strips + pl.program_id(1)
        if turns > 1:
            pl.when(step < relayed)(lambda: far(1, 1, step))
        down = masked(w_down[0], m_down[0])
        part[0] = jnp.dot(units[e], down, preferred_element_type=jnp.float32).astype(jnp.bfloat16)

    pltpu.emit_pipeline(
        down_body,
        grid=(held, strips),
        in_specs=[
            pl.BlockSpec((1, hidden, wide), lambda e, t: (e, 0, t)),
            pl.BlockSpec((1, hidden // BLOCK, wide), lambda e, t: (e, 0, t)),
        ],
        out_specs=[pl.BlockSpec((1, all_rows, wide), lambda e, t: (e, 0, t))],
    )(w_down, m_down, part)

    for d in range(1, turns):
        over(relayed if d == 1 else 0, lambda k: far(1, d, k))
    last(1)
    for kind in (0, 1):
        over(1, lambda k: send_first(kind, k).wait_send())
        for d in range(turns):
            over(0, lambda k: relay(kind, d, k).wait_send())
        for d in range(1, turns):
            over(0, lambda k: cross(kind, d, k).wait_send())


def dispatch(rows_in, cot_in, pick, w_up, m_up, w_down, m_down, scale, owners, groups, span, tile):
    _, packed, piece = rows_in.shape
    _, experts, height, breadth = cot_in.shape
    turns = groups // CORES
    hidden = w_up.shape[2]
    all_rows, width = groups * height, owners * breadth
    return pl.pallas_call(
        functools.partial(dispatch_kernel, owners, groups, span, tile),
        out_shape=(
            jax.ShapeDtypeStruct((experts, all_rows, width), jnp.bfloat16),
            jax.ShapeDtypeStruct((experts, all_rows, width), jnp.bfloat16),
            jax.ShapeDtypeStruct((experts, all_rows, hidden), jnp.bfloat16),
        ),
        in_specs=[pl.BlockSpec(memory_space=pl.ANY)] * 2
        + [pl.BlockSpec(memory_space=pltpu.VMEM)]
        + [pl.BlockSpec(memory_space=pl.ANY)] * 5,
        out_specs=(pl.BlockSpec(memory_space=pl.ANY),) * 3,
        scratch_shapes=[
            pltpu.VMEM((groups * owners, packed, piece), jnp.bfloat16),
            pltpu.VMEM((experts, all_rows, width), jnp.bfloat16),
            pltpu.VMEM((experts, all_rows, hidden), jnp.bfloat16),
            pltpu.SemaphoreType.DMA((2,)),
            pltpu.SemaphoreType.DMA((2, owners)),
            pltpu.SemaphoreType.DMA((2, turns, owners)),
            pltpu.SemaphoreType.DMA((2, turns, owners)),
            pltpu.SemaphoreType.DMA((2, groups, owners)),
        ],
        compiler_params=pltpu.CompilerParams(
            collective_id=0, has_side_effects=True, vmem_limit_bytes=VMEM_LIMIT
        ),
        name="dispatch",
    )(rows_in, cot_in, pick, w_up, m_up, w_down, m_down, scale)


def return_kernel(
    owners, groups, halves, tile, part, grad, w_down, m_down, slope, ret, out, near, sums, far, done,
    near_s, near_r, far_s, far_r, back_s, back_r, local
):
    me, mine = lax.axis_index("dp"), lax.axis_index("expert")
    turns = groups // CORES
    x, core = me // CORES, me % CORES
    other_core = x * CORES + 1 - core
    experts, _, height, width = part.shape
    rows = height // halves
    breadth = width // owners
    chunks = [(e, h) for e in range(experts) for h in range(halves)]
    order = list(range(1, turns)) + [0]

    def band(h):
        return pl.ds(h * rows, rows)

    def fold(e, h, d):
        group = lax.rem(x + d, turns) * CORES + 1 - core
        return pltpu.make_async_remote_copy(
            src_ref=part.at[e, group, band(h)],
            dst_ref=near.at[e, d, band(h)],
            send_sem=near_s.at[e, h, d],
            recv_sem=near_r.at[e, h, d],
            device_id={"dp": other_core, "expert": mine},
            device_id_type=MESH,
        )

    def cross(e, h, d):
        return pltpu.make_async_remote_copy(
            src_ref=sums.at[e, d, band(h)],
            dst_ref=far.at[e, d - 1, band(h)],
            send_sem=far_s.at[e, h, d],
            recv_sem=far_r.at[e, h, d],
            device_id={"dp": lax.rem(x + d, turns) * CORES + core, "expert": mine},
            device_id_type=MESH,
        )

    def columns(owner):
        return pl.ds(pl.multiple_of(owner * breadth, 128), breadth)

    def give(e, h, k):
        peer = lax.rem(mine + k, owners)
        return pltpu.make_async_remote_copy(
            src_ref=done.at[e, band(h), columns(peer)],
            dst_ref=ret.at[mine, e, band(h)],
            send_sem=back_s.at[e, h, k],
            recv_sem=back_r.at[e, h, mine],
            device_id={"dp": me, "expert": peer},
            device_id_type=MESH,
        )

    def keep(e, h):
        return pltpu.make_async_copy(
            done.at[e, band(h), columns(mine)], ret.at[mine, e, band(h)], local.at[e, h]
        )

    def arrival(e, h, source):
        return pltpu.make_async_remote_copy(
            src_ref=done.at[e, band(h), columns(source)],
            dst_ref=ret.at[source, e, band(h)],
            send_sem=back_s.at[e, h, 0],
            recv_sem=back_r.at[e, h, source],
            device_id={"dp": other_core, "expert": mine},
            device_id_type=MESH,
        )

    def over(body):
        def step(k, carry):
            body(k)
            return carry

        lax.fori_loop(1, owners, step, 0)

    greet(owners, groups)
    for e, h in chunks:
        for d in order:
            fold(e, h, d).start()
    def pair(e, h):
        for d in order:
            fold(e, h, d).wait_recv()
            group = lax.rem(x + d, turns) * CORES + core
            sums[e, d, band(h)] = (
                part[e, group, band(h)].astype(jnp.float32)
                + near[e, d, band(h)].astype(jnp.float32)
            ).astype(jnp.bfloat16)
            if d > 0:
                cross(e, h, d).start()

    def finish(e, h):
        total = sums[e, 0, band(h)].astype(jnp.float32)
        for d in range(1, turns):
            cross(e, h, d).wait_recv()
            total = total + far[e, d - 1, band(h)].astype(jnp.float32)
        done[e, band(h)] = total.astype(jnp.bfloat16)
        over(lambda k: give(e, h, k).start())
        keep(e, h).start()

    hidden = slope.shape[2]
    tiles = hidden // tile
    steps = experts * tiles
    duties = [(i // 2, functools.partial(pair, *c)) for i, c in enumerate(chunks)]
    duties += [
        (min(steps - 1, 3 + i), functools.partial(finish, *c)) for i, c in enumerate(chunks)
    ]
    inside = [duty for duty in duties if duty[0] < steps - 1]
    after = [duty for duty in duties if duty[0] >= steps - 1]

    def body(grad, w_down, m_down, slope, out):
        step = pl.program_id(0) * tiles + pl.program_id(1)
        for at, act in inside:
            pl.when(step == at)(act)
        backward_kernel(grad, w_down, m_down, slope, out)

    all_rows = grad.shape[1]
    pltpu.emit_pipeline(
        body,
        grid=(experts, tiles),
        in_specs=[
            pl.BlockSpec((1, all_rows, width), lambda e, t: (e, 0, 0)),
            pl.BlockSpec((1, tile, width), lambda e, t: (e, t, 0)),
            pl.BlockSpec((1, 1, tile // BLOCK, width), lambda e, t: (e, t, 0, 0)),
            pl.BlockSpec((1, all_rows, tile), lambda e, t: (e, 0, t)),
        ],
        out_specs=[pl.BlockSpec((all_rows, tile), lambda e, t: (0, e * tiles + t))],
    )(grad, w_down, m_down, slope, out)
    for _, act in after:
        act()
    for e, h in chunks:
        keep(e, h).wait()
        over(lambda k: arrival(e, h, lax.rem(mine + k, owners)).wait_recv())
        over(lambda k: give(e, h, k).wait_send())
        for d in range(turns):
            fold(e, h, d).wait_send()
        for d in range(1, turns):
            cross(e, h, d).wait_send()


def reduce_return(part, grad, w_down, m_down, slope, owners, tile):
    experts, groups, height, width = part.shape
    turns = groups // CORES
    halves = height // 32 if height % 32 == 0 else 1
    sems = pltpu.SemaphoreType.DMA
    return pl.pallas_call(
        functools.partial(return_kernel, owners, groups, halves, tile),
        out_shape=(
            jax.ShapeDtypeStruct((owners, experts, height, width // owners), jnp.bfloat16),
            jax.ShapeDtypeStruct((slope.shape[1], experts * slope.shape[2]), jnp.bfloat16),
        ),
        in_specs=[pl.BlockSpec(memory_space=pltpu.VMEM)] + [pl.BlockSpec(memory_space=pl.ANY)] * 4,
        out_specs=(pl.BlockSpec(memory_space=pl.ANY),) * 2,
        scratch_shapes=[
            pltpu.VMEM((experts, turns, height, width), jnp.bfloat16),
            pltpu.VMEM((experts, turns, height, width), jnp.bfloat16),
            pltpu.VMEM((experts, max(1, turns - 1), height, width), jnp.bfloat16),
            pltpu.VMEM((experts, height, width), jnp.bfloat16),
            sems((experts, halves, turns)),
            sems((experts, halves, turns)),
            sems((experts, halves, turns)),
            sems((experts, halves, turns)),
            sems((experts, halves, owners)),
            sems((experts, halves, owners)),
            sems((experts, halves)),
        ],
        compiler_params=pltpu.CompilerParams(
            collective_id=1, has_side_effects=True, vmem_limit_bytes=VMEM_LIMIT
        ),
        name="reduce_return",
    )(part, grad, w_down, m_down, slope)


def swap_kernel(owners, give_all, mine_in, out, send, recv):
    me, mine = lax.axis_index("dp"), lax.axis_index("expert")
    barrier = pltpu.get_barrier_semaphore()

    def hail(k, carry):
        peer = lax.rem(mine + k, owners)
        pl.semaphore_signal(
            barrier, inc=1, device_id={"dp": me, "expert": peer}, device_id_type=MESH
        )
        return carry

    def copy(k, source, peer):
        return pltpu.make_async_remote_copy(
            src_ref=mine_in if give_all else mine_in.at[peer],
            dst_ref=out.at[source],
            send_sem=send.at[k],
            recv_sem=recv.at[source],
            device_id={"dp": me, "expert": peer},
            device_id_type=MESH,
        )

    def begin(k, carry):
        copy(k, mine, lax.rem(mine + k, owners)).start()
        return carry

    def end(k, carry):
        peer = lax.rem(mine + k, owners)
        copy(k, peer, peer).wait_recv()
        copy(k, mine, peer).wait_send()
        return carry

    lax.fori_loop(1, owners, hail, 0)
    pl.semaphore_wait(barrier, owners - 1)
    lax.fori_loop(1, owners, begin, 0)
    out[mine] = mine_in[...] if give_all else mine_in[mine]
    lax.fori_loop(1, owners, end, 0)


def swap(values, owners, give_all, number):
    shape = values.shape if give_all else values.shape[1:]
    return pl.pallas_call(
        functools.partial(swap_kernel, owners, give_all),
        out_shape=jax.ShapeDtypeStruct((owners,) + shape, values.dtype),
        in_specs=[pl.BlockSpec(memory_space=pltpu.VMEM)],
        out_specs=pl.BlockSpec(memory_space=pltpu.VMEM),
        scratch_shapes=[
            pltpu.SemaphoreType.DMA((owners,)),
            pltpu.SemaphoreType.DMA((owners,)),
        ],
        compiler_params=pltpu.CompilerParams(collective_id=number, has_side_effects=True),
        name="share" if give_all else "swap",
    )(values)


def masked(weights, mask):
    return (weights.reshape(mask.shape[0], BLOCK, -1) * mask[:, None, :]).reshape(weights.shape)


def backward_kernel(grad, w_down, m_down, slope, out):
    down = masked(w_down[0], m_down[0, 0])
    back = lax.dot_general(
        grad[0], down, (((1,), (1,)), ((), ())), preferred_element_type=jnp.float32
    )
    out[...] = (back * slope[0].astype(jnp.float32)).astype(jnp.bfloat16)


def places(routes, experts, capacity):
    names = jnp.arange(experts, dtype=jnp.int32)
    first, second = [(r[..., None] == names).astype(jnp.bfloat16) for r in routes]
    at = jnp.arange(first.shape[1])
    earlier = jnp.einsum(
        "ab,nbe->nae",
        (at[:, None] > at[None, :]).astype(jnp.bfloat16),
        first + second,
        preferred_element_type=jnp.float32,
    )
    spots = jnp.arange(experts * capacity, dtype=jnp.int32)

    def mark(route, onehot, before):
        slot = jnp.sum(before * onehot.astype(jnp.float32), axis=-1).astype(jnp.int32)
        return ((route * capacity + slot)[..., None] == spots).astype(jnp.bfloat16)

    return (
        mark(routes[0], first, earlier),
        mark(routes[1], second, earlier + first.astype(jnp.float32)),
    )


def shards(
    tokens, routes, gate_fixed, up_weight, up_mask, down_weight, down_mask, threshold, cotangent
):
    owners = lax.axis_size("expert")
    groups = lax.axis_size("dp")
    tok_rows, width = tokens.shape
    held, _, hidden = up_weight.shape
    experts = held * owners
    capacity = (tok_rows * 5 + 2 * experts - 1) // (2 * experts)
    blocks = owners * groups
    all_rows = blocks * capacity
    height = owners * capacity
    breadth = width // owners
    pieces = 1
    while (held * capacity * pieces) % 16:
        pieces *= 2
    piece = width // pieces
    span = 1
    while (span * capacity) % 16:
        span *= 2
    tile = 256 if hidden % 256 == 0 else BLOCK
    tiles = hidden // tile

    table = jnp.concatenate([routes, gate_fixed], axis=1).T
    own = places((table[None, 0], table[None, 1]), experts, capacity)
    choose = (own[0] + own[1]).reshape(tok_rows, owners, held * capacity)
    rows_in = jnp.concatenate(
        [
            jnp.einsum(
                "top,td->opd",
                choose,
                tokens[:, q * piece:(q + 1) * piece],
                preferred_element_type=jnp.float32,
            ).astype(jnp.bfloat16)
            for q in range(pieces)
        ],
        axis=1,
    )

    known = swap(table, owners, True, 2)
    marks = places((known[:, 0], known[:, 1]), experts, capacity)
    gates = [known[:, 2 + k].astype(jnp.float32)[..., None] / 65536.0 for k in range(2)]
    cot = cotangent.reshape(owners, tok_rows, breadth).astype(jnp.float32)
    cot_in = sum(
        jnp.einsum(
            "btp,btd->bpd",
            mark,
            (gate * cot).astype(jnp.bfloat16),
            preferred_element_type=jnp.float32,
        )
        for mark, gate in zip(marks, gates)
    ).astype(jnp.bfloat16)
    cot_in = cot_in.reshape(owners, owners, held, capacity, breadth).transpose(1, 2, 0, 3, 4)
    cot_in = cot_in.reshape(owners, held, height, breadth)

    sources = np.arange(span * pieces * held * capacity)
    expert_of = sources // capacity % held
    piece_of = sources // (capacity * held) % pieces
    block_of = sources // (capacity * held * pieces)
    target = (expert_of * span + block_of) * capacity + sources % capacity
    pick = jnp.asarray(
        (piece_of == np.arange(pieces)[:, None, None])
        & (target == np.arange(held * span * capacity)[:, None]),
        jnp.bfloat16,
    )

    scale = (4.0 / threshold.astype(jnp.float32)).reshape(held, 1, hidden)
    wide_up = jnp.repeat(up_mask.astype(jnp.bfloat16), BLOCK, axis=2)
    wide_down = jnp.repeat(down_mask.astype(jnp.bfloat16), BLOCK, axis=2)
    grad_rows, part, slope = dispatch(
        rows_in, cot_in, pick, up_weight, wide_up, down_weight, wide_down, scale,
        owners, groups, span, tile,
    )
    ret, potential_grad = reduce_return(
        part.reshape(held, groups, height, width),
        grad_rows, down_weight, wide_down.reshape(held, tiles, tile // BLOCK, width),
        slope, owners, tile,
    )
    potential_grad = potential_grad.reshape(all_rows, held, hidden)

    by_block = ret.reshape(owners, held, owners, capacity, breadth).transpose(2, 0, 1, 3, 4)
    by_block = by_block.reshape(owners, experts * capacity, breadth)
    picked = [
        jnp.einsum("btp,bpd->btd", mark, by_block, preferred_element_type=jnp.float32)
        for mark in marks
    ]
    mixed = (gates[0] * picked[0] + gates[1] * picked[1]).astype(jnp.bfloat16)
    mixed = mixed.reshape(owners * tok_rows, breadth)
    gate_part = jnp.stack([jnp.sum(cot * p, axis=2) for p in picked], axis=1)
    gate_grad = jnp.sum(swap(gate_part, owners, False, 3), axis=0).T
    return (mixed, gate_grad * (1.0 / math.sqrt(width)), potential_grad)


def solution(mesh):
    placed = (
        P(("dp", "expert"), None),
        P(("dp", "expert"), None),
        P(("dp", "expert"), None),
        P("expert", None, "dp"),
        P("expert", None, "dp"),
        P("expert", "dp", None),
        P("expert", "dp", None),
        P("expert", "dp"),
        P("dp", "expert"),
    )
    return jax.shard_map(
        shards,
        mesh=mesh,
        in_specs=placed,
        out_specs=(P("dp", "expert"), P(("dp", "expert"), None), P(None, "expert", "dp")),
        check_vma=False,
    )
```
